256 devices in a mesh: slab: 4 (over x), grp: 64 (over y, z, core).
Axes of the slice: x: 4, y: 4, z: 8, core: 2. Of those that a mesh axis runs over, the one named last changes fastest.
Arguments:
- contact_jac: float32 [16384, 3, 64, 128], P(('slab', 'grp')), may hold values from -0.5 to 0.5
- contact_bodies: int32 [16384, 2], P(('slab', 'grp')), may hold values from 0 to 2047
- contact_class: int32 [16384, 64], P(('slab', 'grp')), may hold values from 0 to 7
- contact_count: int32 [256], P(('slab', 'grp')), may hold values from 16 to 64, as said below
- face_jac: float32 [4096, 3, 64, 128], P(('slab', 'grp')), may hold values from -0.5 to 0.5
- face_own: int32 [4096], P(('slab', 'grp')), may hold values from 0 to 2047
- face_far: int32 [4096], P(('slab', 'grp')), may hold values from 0 to 2047
- face_class: int32 [4096, 64], P(('slab', 'grp')), may hold values from 0 to 7
- warm_contact: float32 [16384, 192], P(('slab', 'grp')), may hold values from -6 to 6
- warm_face: float32 [4096, 192], P(('slab', 'grp')), may hold values from -6 to 6
- free_velocity: float32 [524288], P(('slab', 'grp')), may hold values from -6 to 6
- inverse_mass: float32 [524288], P(('slab', 'grp')), may hold values from 0.25 to 4
- friction_table: float32 [8], replicated, may hold values from 0.1 to 1
- first_step: float32 [1], replicated, may hold values from 0.05 to 0.2
Outputs:
- contact_impulse: float32 [16384, 192], P(('slab', 'grp'))
- face_impulse: float32 [4096, 192], P(('slab', 'grp'))
- body_velocity: float32 [524288], P(('slab', 'grp'))
The draws below stay inside these ranges and needn't reach their ends.
Inputs may be any that keep to these rules, and one draw needn't show every extreme that they name: `contact_count`: 64 on some device in every draw.
All inputs are finite; a program needn't handle non-finite values.
Results may differ from the reference program's by a relative error of at most 0.0003.
Values sent between devices are 32-bit elements; how exact they have to be, the bound alone decides.
No kernel may reach another device: no remote copies, remote signals or barrier semaphores. Data moves between devices by JAX's collectives and lax.ppermute only.
A program may use at most 64 MiB of HBM per device.

```python
import math
import jax
import jax.numpy as jnp
from jax import lax

BLK = 64
COMP = 3
NCLASS = 8
ITERS = 3
KB_DEV = 64
FB_DEV = 16
PANEL = 2048
KB_ALL = 16384
FB_ALL = 4096
BODY_DOF = 524288
N_SLAB = 4
N_GRP = 64


def draw_contact_count(key, part):
    key = jax.random.fold_in(key, 11)
    key_base, key_full, key_pick = jax.random.split(key, 3)
    devices_all = N_SLAB * N_GRP
    base = jax.random.randint(key_base, (devices_all,), max(1, KB_DEV // 4), KB_DEV // 2 + 1)
    full = jax.random.randint(key_full, (devices_all,), 0, 8) == 0
    picked = jax.random.randint(key_pick, (), 0, devices_all)
    full = jnp.logical_or(full, jnp.arange(devices_all) == picked)
    return jnp.where(full, KB_DEV, base).astype(jnp.int32)


def plant(result, stream_key, low, top_value):
    longest = result.shape.index(max(result.shape))
    spots = []
    for shift in (0, 1):
        where = [jax.random.randint(jax.random.fold_in(stream_key, axis), (), 0, length) for axis, length in enumerate(result.shape)]
        where[longest] = (where[longest] + shift) % result.shape[longest]
        spots.append(tuple(where))
    return result.at[spots[0]].set(low).at[spots[1]].set(top_value)


def block_levels(rng, extent, cuts, smallest, high):
    gain, own = 1.0, jax.random.fold_in(rng, 6)
    for axis_at, shards_of in cuts:
        steps = jnp.exp(jax.random.uniform(jax.random.fold_in(own, axis_at), (shards_of,), jnp.float32, smallest / len(cuts), high / len(cuts)))
        gain = gain * jnp.repeat(steps, extent[axis_at] // shards_of).reshape([-1 if axis == axis_at else 1 for axis in range(len(extent))])
    return gain


def normal_values(key, dims, scale, most, cuts=(), held_as=jnp.bfloat16):
    values = jax.random.normal(key, dims, jnp.float32) * scale
    if len(cuts) > 0:
        values = block_levels(key, dims, cuts, -0.22, 0.18) * values
    return jnp.clip(values, min=-most, max=most).astype(held_as)


def setup_inputs(seed: int = 0) -> dict:
    splits = jax.random.split(jax.random.key(seed), 15)
    return {
        "contact_jac": normal_values(splits[0], (KB_ALL, COMP, BLK, 2 * BLK), (2 * BLK) ** -0.5, 0.5, ((0, 256),), jnp.float32),
        "contact_bodies": plant(jax.random.randint(splits[1], (KB_ALL, 2), 0, PANEL), jax.random.fold_in(splits[1], 1), 0, PANEL - 1).astype(jnp.int32),
        "contact_class": plant(jax.random.randint(splits[2], (KB_ALL, BLK), 0, NCLASS), jax.random.fold_in(splits[2], 1), 0, NCLASS - 1).astype(jnp.int32),
        "contact_count": draw_contact_count(jax.random.fold_in(splits[14], 71), 0),
        "face_jac": normal_values(splits[4], (FB_ALL, COMP, BLK, 2 * BLK), (2 * BLK) ** -0.5, 0.5, ((0, 256),), jnp.float32),
        "face_own": plant(jax.random.randint(splits[5], (FB_ALL,), 0, PANEL), jax.random.fold_in(splits[5], 1), 0, PANEL - 1).astype(jnp.int32),
        "face_far": plant(jax.random.randint(splits[6], (FB_ALL,), 0, PANEL), jax.random.fold_in(splits[6], 1), 0, PANEL - 1).astype(jnp.int32),
        "face_class": plant(jax.random.randint(splits[7], (FB_ALL, BLK), 0, NCLASS), jax.random.fold_in(splits[7], 1), 0, NCLASS - 1).astype(jnp.int32),
        "warm_contact": normal_values(splits[8], (KB_ALL, COMP * BLK), 1.0, 6.0, ((0, 256),), jnp.float32),
        "warm_face": normal_values(splits[9], (FB_ALL, COMP * BLK), 1.0, 6.0, ((0, 256),), jnp.float32),
        "free_velocity": normal_values(splits[10], (BODY_DOF,), 1.0, 6.0, ((0, 256),), jnp.float32),
        "inverse_mass": jnp.clip(jnp.exp(math.log(4.0) - 2.7725887 * jax.random.uniform(splits[11], (BODY_DOF,), jnp.float32) ** block_levels(splits[11], (BODY_DOF,), ((0, 256),), -0.2, 0.2)), 0.25, 4.0),
        "friction_table": jnp.clip(jax.random.uniform(splits[12], (NCLASS,), jnp.float32, 0.1, 1.0), 0.1, 1.0),
        "first_step": jnp.clip(jnp.exp(jax.random.uniform(splits[13], (1,), jnp.float32, math.log(0.05), math.log(0.2))), 0.05, 0.2),
    }


regular_weight = 0.05
tiny_sum = 1e-06

def momentum_weights(count):
    theta = 1.0
    weights = []
    for turn in range(count):
        following = (theta * math.sqrt(theta * theta + 4.0) - theta * theta) / 2.0
        weights.append(theta * (1.0 - theta) / (theta * theta + following))
        theta = following
    return weights

def cone_project(pushed, friction, width):
    normal = pushed[:, :width]
    first = pushed[:, width:2 * width]
    second = pushed[:, 2 * width:]
    tangent = jnp.sqrt(first * first + second * second)
    inside = tangent <= friction * normal
    vanish = friction * tangent <= -normal
    onto = jnp.logical_not(jnp.logical_or(inside, vanish))
    normal_new = (friction * tangent + normal) / (friction * friction + 1.0)
    ratio = jnp.where(onto, friction * normal_new / jnp.where(onto, tangent, 1.0), 1.0)
    keep = jnp.where(inside, 1.0, jnp.where(vanish, 0.0, ratio))
    normal_out = jnp.where(inside, normal, jnp.where(vanish, 0.0, normal_new))
    return jnp.concatenate([normal_out, first * keep, second * keep], 1)

def reference(contact_jac, contact_bodies, contact_class, contact_count, face_jac, face_own, face_far, face_class, warm_contact, warm_face, free_velocity, inverse_mass, friction_table, first_step):
    highest = lax.Precision.HIGHEST
    contact_rows = contact_jac.shape[0]
    face_rows = face_jac.shape[0]
    slots = jnp.arange(contact_rows, dtype=jnp.int32)
    owner = slots // KB_DEV
    offset = owner // N_GRP * PANEL
    body_first = offset + contact_bodies[:, 0]
    body_second = offset + contact_bodies[:, 1]
    live = (slots % KB_DEV < contact_count[owner]).astype(jnp.float32)[:, None]
    face_slots = jnp.arange(face_rows, dtype=jnp.int32)
    face_slab = face_slots // (FB_DEV * N_GRP)
    body_own = face_slab * PANEL + face_own
    far_row = (face_slots + N_GRP * FB_DEV) % face_rows
    body_far = (face_slab + 1) % N_SLAB * PANEL + face_far[far_row]
    friction_contact = friction_table[contact_class]
    friction_face = friction_table[face_class]
    block_count = N_SLAB * PANEL

    def velocity_of(contact_y, face_y):
        contact_terms = jnp.einsum('kcij,kci->kj', contact_jac, contact_y.reshape(contact_rows, COMP, BLK), precision=highest)
        face_terms = jnp.einsum('kcij,kci->kj', face_jac, face_y.reshape(face_rows, COMP, BLK), precision=highest)
        total = jnp.zeros((block_count, BLK), jnp.float32)
        total = total.at[body_first].add(contact_terms[:, :BLK])
        total = total.at[body_second].add(contact_terms[:, BLK:])
        total = total.at[body_own].add(face_terms[:, :BLK])
        total = total.at[body_far].add(face_terms[:, BLK:])
        return free_velocity + inverse_mass * total.reshape(-1)

    def gradients(velocity, contact_y, face_y):
        blocks = velocity.reshape(block_count, BLK)
        joined = jnp.concatenate([blocks[body_first], blocks[body_second]], 1)
        contact_grad = jnp.einsum('kcij,kj->kci', contact_jac, joined, precision=highest).reshape(contact_rows, COMP * BLK)
        contact_grad = (contact_grad + regular_weight * contact_y) * live
        face_joined = jnp.concatenate([blocks[body_own], blocks[body_far]], 1)
        face_grad = jnp.einsum('kcij,kj->kci', face_jac, face_joined, precision=highest).reshape(face_rows, COMP * BLK)
        face_grad = face_grad + regular_weight * face_y
        return (contact_grad, face_grad)
    betas = momentum_weights(ITERS)
    contact_now = warm_contact * live
    face_now = warm_face
    contact_y, face_y = (contact_now, face_now)
    last_cy, last_fy, last_cg, last_fg = (contact_y, face_y, contact_y, face_y)
    for turn in range(ITERS):
        velocity = velocity_of(contact_y, face_y)
        contact_grad, face_grad = gradients(velocity, contact_y, face_y)
        if turn == 0:
            step = first_step[0]
        else:
            change_c = contact_y - last_cy
            change_f = face_y - last_fy
            spread = jnp.sum(change_c * change_c) + jnp.sum(change_f * change_f)
            curve = jnp.sum(change_c * (contact_grad - last_cg)) + jnp.sum(change_f * (face_grad - last_fg))
            step = (spread + tiny_sum) / (curve + tiny_sum)
        contact_new = cone_project(contact_y - step * contact_grad, friction_contact, BLK) * live
        face_new = cone_project(face_y - step * face_grad, friction_face, BLK)
        last_cy, last_fy, last_cg, last_fg = (contact_y, face_y, contact_grad, face_grad)
        contact_y = contact_new + betas[turn] * (contact_new - contact_now)
        face_y = face_new + betas[turn] * (face_new - face_now)
        contact_now, face_now = (contact_new, face_new)
    return (contact_now, face_now, velocity_of(contact_now, face_now))
```

```python
import math

import jax
import jax.numpy as jnp
from jax import lax
from jax.sharding import PartitionSpec as P

BLK = 64
COMP = 3
ITERS = 3
NY, NZ, NC = 4, 8, 2
OWN = 16


regular_weight = 0.05
tiny_sum = 1e-06


def shifted(x, axis, by):
    devices = lax.axis_size(axis)
    return lax.ppermute(x, axis, [(i, (i + by) % devices) for i in range(devices)])


def moved(x, dy, dz, dc):
    pairs = []
    for y in range(NY):
        for z in range(NZ):
            for c in range(NC):
                here = (y * NZ + z) * NC + c
                there = (((y + dy) % NY) * NZ + (z + dz) % NZ) * NC + (c + dc) % NC
                pairs.append((here, there))
    return lax.ppermute(x, "grp", pairs)


def momentum_weights(count):
    theta = 1.0
    weights = []
    for turn in range(count):
        following = (theta * math.sqrt(theta * theta + 4.0) - theta * theta) / 2.0
        weights.append(theta * (1.0 - theta) / (theta * theta + following))
        theta = following
    return weights


def cone_project(pushed, friction, width):
    normal = pushed[:, :width]
    first = pushed[:, width : 2 * width]
    second = pushed[:, 2 * width :]
    tangent = jnp.sqrt(first * first + second * second)
    inside = tangent <= friction * normal
    vanish = friction * tangent <= -normal
    onto = jnp.logical_not(jnp.logical_or(inside, vanish))
    normal_new = (friction * tangent + normal) / (friction * friction + 1.0)
    ratio = jnp.where(onto, friction * normal_new / jnp.where(onto, tangent, 1.0), 1.0)
    keep = jnp.where(inside, 1.0, jnp.where(vanish, 0.0, ratio))
    normal_out = jnp.where(inside, normal, jnp.where(vanish, 0.0, normal_new))
    return jnp.concatenate([normal_out, first * keep, second * keep], 1)


def class_lookup(classes, table):
    levels = jnp.arange(table.shape[0], dtype=jnp.int32)
    picked = (classes[:, :, None] == levels).astype(jnp.float32)
    return jnp.sum(picked * table, axis=2)


def relative_slot(block):
    me = lax.axis_index("grp")
    owner = block // (2 * OWN)
    dc = (owner - me) % NC
    dz = (owner // NC - me // NC) % NZ
    dy = (owner // (NC * NZ) - me // (NC * NZ)) % NY
    return (dc * NY + dy) * NZ + dz


def reduce_scatter(panel):
    half = panel[0] + moved(panel[1], 0, 0, 1)
    parts = [moved(half[dy], dy, 0, 0) for dy in range(1, NY)]
    strip = half[0] + sum(parts)
    parts = [moved(strip[dz], 0, dz, 0) for dz in range(1, NZ)]
    return strip[0] + sum(parts)


def all_gather(piece):
    strip = jnp.stack([piece] + [moved(piece, 0, -dz, 0) for dz in range(1, NZ)])
    half = jnp.stack([strip] + [moved(strip, -dy, 0, 0) for dy in range(1, NY)])
    return jnp.stack([half, moved(half, 0, 0, 1)])


def on_device(
    contact_jac,
    contact_bodies,
    contact_class,
    contact_count,
    face_jac,
    face_own,
    face_far,
    face_class,
    warm_contact,
    warm_face,
    free_velocity,
    inverse_mass,
    friction_table,
    first_step,
):
    highest = lax.Precision.HIGHEST
    contact_rows = contact_jac.shape[0]
    face_rows = face_jac.shape[0]
    free_own = free_velocity.reshape(OWN, 128)
    mass_own = inverse_mass.reshape(OWN, 128)
    slots = jnp.arange(contact_rows, dtype=jnp.int32)
    live = (slots < contact_count[0]).astype(jnp.float32)[:, None]
    targets = jnp.concatenate(
        [contact_bodies[:, 0], contact_bodies[:, 1], face_own, face_far]
    )
    target_slot = relative_slot(targets)
    target_row = (targets % (2 * OWN)) // 2
    target_odd = (targets % 2 == 1)[:, None]
    friction_contact = class_lookup(contact_class, friction_table)
    friction_face = class_lookup(face_class, friction_table)

    def owned_force(contact_y, face_y):
        face_terms = jnp.einsum(
            "kcij,kci->kj", face_jac, face_y.reshape(face_rows, COMP, BLK), precision=highest
        )
        arriving = shifted(face_terms[:, BLK:], "slab", 1)
        contact_terms = jnp.einsum(
            "kcij,kci->kj",
            contact_jac,
            contact_y.reshape(contact_rows, COMP, BLK),
            precision=highest,
        )
        rows = jnp.concatenate(
            [contact_terms[:, :BLK], contact_terms[:, BLK:], face_terms[:, :BLK], arriving]
        )
        wide = jnp.concatenate(
            [jnp.where(target_odd, 0.0, rows), jnp.where(target_odd, rows, 0.0)], 1
        )
        total = jnp.zeros((NC * NY * NZ * OWN, 128), jnp.float32)
        total = total.at[target_slot * OWN + target_row].add(wide)
        return reduce_scatter(total.reshape(NC, NY, NZ, OWN, 128))

    betas = momentum_weights(ITERS)
    contact_now = warm_contact * live
    face_now = warm_face
    contact_y, face_y = (contact_now, face_now)
    last_cy, last_fy, last_owned = (contact_y, face_y, None)
    for turn in range(ITERS):
        if turn > 0:
            change_c = contact_y - last_cy
            change_f = face_y - last_fy
            spread = jnp.sum(change_c * change_c) + jnp.sum(change_f * change_f)
        owned = owned_force(contact_y, face_y)
        piece = free_own + mass_own * owned
        if turn > 0:
            change = owned - last_owned
            curve = jnp.sum(mass_own * change * change)
            row = lax.broadcasted_iota(jnp.int32, (8, 128), 0)
            sums = jnp.where(row == 0, spread, curve)
            piece = jnp.concatenate([piece, sums], 0)
        gathered = all_gather(piece)
        rows = gathered.shape[3]
        if turn > 0:
            slab_sums = jnp.sum(gathered[:, :, :, OWN:, :], (0, 1, 2))
            others = [shifted(slab_sums, "slab", by) for by in (1, 2, 3)]
        picked = gathered.reshape(-1, 128)[target_slot * rows + target_row]
        blocks = jnp.where(target_odd, picked[:, BLK:], picked[:, :BLK])
        at = contact_rows
        returning = shifted(blocks[2 * at + face_rows :], "slab", -1)
        joined = jnp.concatenate([blocks[:at], blocks[at : 2 * at]], 1)
        contact_grad = jnp.einsum("kcij,kj->kci", contact_jac, joined, precision=highest).reshape(
            contact_rows, COMP * BLK
        )
        contact_grad = (contact_grad + regular_weight * contact_y) * live
        face_joined = jnp.concatenate([blocks[2 * at : 2 * at + face_rows], returning], 1)
        face_grad = jnp.einsum("kcij,kj->kci", face_jac, face_joined, precision=highest).reshape(
            face_rows, COMP * BLK
        )
        face_grad = face_grad + regular_weight * face_y
        if turn == 0:
            step = first_step[0]
        else:
            sums = slab_sums + sum(others)
            spread, curve = sums[0, 0], sums[1, 0]
            curve = curve + regular_weight * spread
            step = (spread + tiny_sum) / (curve + tiny_sum)
        contact_new = cone_project(contact_y - step * contact_grad, friction_contact, BLK) * live
        face_new = cone_project(face_y - step * face_grad, friction_face, BLK)
        last_cy, last_fy, last_owned = (contact_y, face_y, owned)
        contact_y = contact_new + betas[turn] * (contact_new - contact_now)
        face_y = face_new + betas[turn] * (face_new - face_now)
        contact_now, face_now = (contact_new, face_new)
    owned_final = owned_force(contact_now, face_now)
    final = free_own + mass_own * owned_final
    return (contact_now, face_now, final.reshape(-1))


def solution(mesh):
    return jax.shard_map(
        on_device,
        mesh=mesh,
        in_specs=(
            P(("slab", "grp"), None, None, None),
            P(("slab", "grp"), None),
            P(("slab", "grp"), None),
            P(("slab", "grp")),
            P(("slab", "grp"), None, None, None),
            P(("slab", "grp")),
            P(("slab", "grp")),
            P(("slab", "grp"), None),
            P(("slab", "grp"), None),
            P(("slab", "grp"), None),
            P(("slab", "grp")),
            P(("slab", "grp")),
            P(),
            P(),
        ),
        out_specs=(P(("slab", "grp"), None), P(("slab", "grp"), None), P(("slab", "grp"))),
        check_vma=False,
    )
```

```python
import math

import jax
import jax.numpy as jnp
from jax import lax
from jax.sharding import PartitionSpec as P

BLK = 64
COMP = 3
ITERS = 3
NY, NZ, NC = 4, 8, 2
OWN = 16


regular_weight = 0.05
tiny_sum = 1e-06


def shifted(x, axis, by):
    devices = lax.axis_size(axis)
    return lax.ppermute(x, axis, [(i, (i + by) % devices) for i in range(devices)])


def moved(x, dy, dz, dc):
    pairs = []
    for y in range(NY):
        for z in range(NZ):
            for c in range(NC):
                here = (y * NZ + z) * NC + c
                there = (((y + dy) % NY) * NZ + (z + dz) % NZ) * NC + (c + dc) % NC
                pairs.append((here, there))
    return lax.ppermute(x, "grp", pairs)


def momentum_weights(count):
    theta = 1.0
    weights = []
    for turn in range(count):
        following = (theta * math.sqrt(theta * theta + 4.0) - theta * theta) / 2.0
        weights.append(theta * (1.0 - theta) / (theta * theta + following))
        theta = following
    return weights


def cone_project(pushed, friction, width):
    normal = pushed[:, :width]
    first = pushed[:, width : 2 * width]
    second = pushed[:, 2 * width :]
    tangent = jnp.sqrt(first * first + second * second)
    inside = tangent <= friction * normal
    vanish = friction * tangent <= -normal
    onto = jnp.logical_not(jnp.logical_or(inside, vanish))
    normal_new = (friction * tangent + normal) / (friction * friction + 1.0)
    ratio = jnp.where(onto, friction * normal_new / jnp.where(onto, tangent, 1.0), 1.0)
    keep = jnp.where(inside, 1.0, jnp.where(vanish, 0.0, ratio))
    normal_out = jnp.where(inside, normal, jnp.where(vanish, 0.0, normal_new))
    return jnp.concatenate([normal_out, first * keep, second * keep], 1)


def class_lookup(classes, table):
    levels = jnp.arange(table.shape[0], dtype=jnp.int32)
    picked = (classes[:, :, None] == levels).astype(jnp.float32)
    return jnp.sum(picked * table, axis=2)


def relative_slot(block):
    owner = block // (2 * OWN)
    dc = (owner - lax.axis_index("grp")) % NC
    return dc * (NY * NZ) + owner // NC


def exchange(parts):
    groups = [[chip * NC + core for chip in range(NY * NZ)] for core in range(NC)]
    return lax.all_to_all(parts, "grp", 0, 0, axis_index_groups=groups, tiled=True)


def reduce_scatter(panel):
    half = panel[0] + moved(panel[1], 0, 0, 1)
    return jnp.sum(exchange(half), 0)


def all_gather(piece):
    half = exchange(jnp.broadcast_to(piece, (NY * NZ,) + piece.shape))
    return jnp.stack([half, moved(half, 0, 0, 1)])


def on_device(
    contact_jac,
    contact_bodies,
    contact_class,
    contact_count,
    face_jac,
    face_own,
    face_far,
    face_class,
    warm_contact,
    warm_face,
    free_velocity,
    inverse_mass,
    friction_table,
    first_step,
):
    highest = lax.Precision.HIGHEST
    contact_rows = contact_jac.shape[0]
    face_rows = face_jac.shape[0]
    free_own = free_velocity.reshape(OWN, 128)
    mass_own = inverse_mass.reshape(OWN, 128)
    slots = jnp.arange(contact_rows, dtype=jnp.int32)
    live = (slots < contact_count[0]).astype(jnp.float32)[:, None]
    targets = jnp.concatenate(
        [contact_bodies[:, 0], contact_bodies[:, 1], face_own, face_far]
    )
    target_slot = relative_slot(targets)
    target_row = (targets % (2 * OWN)) // 2
    target_odd = (targets % 2 == 1)[:, None]
    friction_contact = class_lookup(contact_class, friction_table)
    friction_face = class_lookup(face_class, friction_table)

    def owned_force(contact_y, face_y):
        face_terms = jnp.einsum(
            "kcij,kci->kj", face_jac, face_y.reshape(face_rows, COMP, BLK), precision=highest
        )
        arriving = shifted(face_terms[:, BLK:], "slab", 1)
        contact_terms = jnp.einsum(
            "kcij,kci->kj",
            contact_jac,
            contact_y.reshape(contact_rows, COMP, BLK),
            precision=highest,
        )
        rows = jnp.concatenate(
            [contact_terms[:, :BLK], contact_terms[:, BLK:], face_terms[:, :BLK], arriving]
        )
        wide = jnp.concatenate(
            [jnp.where(target_odd, 0.0, rows), jnp.where(target_odd, rows, 0.0)], 1
        )
        total = jnp.zeros((NC * NY * NZ * OWN, 128), jnp.float32)
        total = total.at[target_slot * OWN + target_row].add(wide)
        return reduce_scatter(total.reshape(NC, NY * NZ, OWN, 128))

    betas = momentum_weights(ITERS)
    contact_now = warm_contact * live
    face_now = warm_face
    contact_y, face_y = (contact_now, face_now)
    last_cy, last_fy, last_owned = (contact_y, face_y, None)
    for turn in range(ITERS):
        if turn > 0:
            change_c = contact_y - last_cy
            change_f = face_y - last_fy
            spread = jnp.sum(change_c * change_c) + jnp.sum(change_f * change_f)
        owned = owned_force(contact_y, face_y)
        piece = free_own + mass_own * owned
        if turn > 0:
            change = owned - last_owned
            curve = jnp.sum(mass_own * change * change)
            row = lax.broadcasted_iota(jnp.int32, (8, 128), 0)
            sums = jnp.where(row == 0, spread, curve)
            piece = jnp.concatenate([piece, sums], 0)
        gathered = all_gather(piece)
        rows = gathered.shape[2]
        if turn > 0:
            slab_sums = jnp.sum(gathered[:, :, OWN:, :], (0, 1))
            others = [shifted(slab_sums, "slab", by) for by in (1, 2, 3)]
        picked = gathered.reshape(-1, 128)[target_slot * rows + target_row]
        blocks = jnp.where(target_odd, picked[:, BLK:], picked[:, :BLK])
        at = contact_rows
        returning = shifted(blocks[2 * at + face_rows :], "slab", -1)
        joined = jnp.concatenate([blocks[:at], blocks[at : 2 * at]], 1)
        contact_grad = jnp.einsum("kcij,kj->kci", contact_jac, joined, precision=highest).reshape(
            contact_rows, COMP * BLK
        )
        contact_grad = (contact_grad + regular_weight * contact_y) * live
        face_joined = jnp.concatenate([blocks[2 * at : 2 * at + face_rows], returning], 1)
        face_grad = jnp.einsum("kcij,kj->kci", face_jac, face_joined, precision=highest).reshape(
            face_rows, COMP * BLK
        )
        face_grad = face_grad + regular_weight * face_y
        if turn == 0:
            step = first_step[0]
        else:
            sums = slab_sums + sum(others)
            spread, curve = sums[0, 0], sums[1, 0]
            curve = curve + regular_weight * spread
            step = (spread + tiny_sum) / (curve + tiny_sum)
        contact_new = cone_project(contact_y - step * contact_grad, friction_contact, BLK) * live
        face_new = cone_project(face_y - step * face_grad, friction_face, BLK)
        last_cy, last_fy, last_owned = (contact_y, face_y, owned)
        contact_y = contact_new + betas[turn] * (contact_new - contact_now)
        face_y = face_new + betas[turn] * (face_new - face_now)
        contact_now, face_now = (contact_new, face_new)
    owned_final = owned_force(contact_now, face_now)
    final = free_own + mass_own * owned_final
    return (contact_now, face_now, final.reshape(-1))


def solution(mesh):
    return jax.shard_map(
        on_device,
        mesh=mesh,
        in_specs=(
            P(("slab", "grp"), None, None, None),
            P(("slab", "grp"), None),
            P(("slab", "grp"), None),
            P(("slab", "grp")),
            P(("slab", "grp"), None, None, None),
            P(("slab", "grp")),
            P(("slab", "grp")),
            P(("slab", "grp"), None),
            P(("slab", "grp"), None),
            P(("slab", "grp"), None),
            P(("slab", "grp")),
            P(("slab", "grp")),
            P(),
            P(),
        ),
        out_specs=(P(("slab", "grp"), None), P(("slab", "grp"), None), P(("slab", "grp"))),
        check_vma=False,
    )
```

```python
import functools
import math

import jax
import jax.numpy as jnp
from jax import lax
from jax.experimental import pallas as pl
from jax.experimental.pallas import tpu as pltpu
from jax.sharding import PartitionSpec as P

BLK = 64
COMP = 3
ITERS = 3
NY, NZ, NC = 4, 8, 2
CHIPS = NY * NZ
OWN = 16

KC, KF = 64, 16
GC, GF = 128 // KC, 128 // KF
IC, IF = BLK // GC, BLK // GF
SC, SF = COMP * IC, COMP * IF

regular_weight = 0.05
tiny_sum = 1e-06
vmem = pl.BlockSpec(memory_space=pltpu.VMEM)
smem = pl.BlockSpec(memory_space=pltpu.SMEM)
hbm = pl.BlockSpec(memory_space=pltpu.HBM)
f32 = jnp.float32


def shape(*dims):
    return jax.ShapeDtypeStruct(dims, f32)


def kernel_call(body, out, specs, scratch=(), megabytes=4, out_specs=None):
    return pl.pallas_call(
        body,
        out_shape=out,
        in_specs=specs,
        out_specs=out_specs or jax.tree.map(lambda _: vmem, out),
        scratch_shapes=list(scratch),
        compiler_params=pltpu.CompilerParams(vmem_limit_bytes=megabytes << 20),
    )


def shifted(x, axis, by):
    devices = lax.axis_size(axis)
    return lax.ppermute(x, axis, [(i, (i + by) % devices) for i in range(devices)])


def other_core(x):
    devices = CHIPS * NC
    return lax.ppermute(x, "grp", [(i, i ^ 1) for i in range(devices)])


def momentum_weights(count):
    theta = 1.0
    weights = []
    for turn in range(count):
        following = (theta * math.sqrt(theta * theta + 4.0) - theta * theta) / 2.0
        weights.append(theta * (1.0 - theta) / (theta * theta + following))
        theta = following
    return weights


def class_lookup(classes, table):
    levels = jnp.arange(table.shape[0], dtype=jnp.int32)
    picked = (classes[:, :, None] == levels).astype(f32)
    return jnp.sum(picked * table, axis=2)


def to_lanes(x, parts):
    k, width = x.shape
    x = x.reshape(k, width // BLK, parts, BLK // parts)
    return x.transpose(1, 3, 2, 0).reshape(width // parts, 128)


def from_lanes(x, parts):
    x = x.reshape(-1, BLK // parts, parts, 128 // parts)
    return x.transpose(3, 0, 2, 1).reshape(128 // parts, -1)


def left_half(rows):
    return lax.broadcasted_iota(jnp.int32, (rows, 128), 1) < BLK


def rows_of(slice_at):
    return pl.ds(pl.multiple_of(slice_at * 128, 128), 128)


def accumulate(jac, y, first, count, total):
    def add(s, total):
        return total + jac[rows_of(s), :] * y[pl.ds(s, 1), :]

    return lax.fori_loop(first, first + count, add, total, unroll=4)


def folded(total, parts):
    turned = total.T
    k = 128 // parts
    return sum(turned[p * k : (p + 1) * k] for p in range(parts))


def product(jac, velocity, partial, first, count):
    def one(s, _):
        terms = jac[rows_of(s), :] * velocity
        partial[pl.ds(pl.multiple_of(s * 8, 8), 8), :] = jnp.sum(
            terms.reshape(16, 8, 128), axis=0
        )
        return _

    lax.fori_loop(first, first + count, one, 0, unroll=4)


def summed(partial, slices):
    return sum(partial[pl.ds(q, slices, stride=8), :] for q in range(8))


def first_force_kernel(cjac, fjac, cwarm, fwarm, terms, cbuf, fbuf, partial, csem, fsem):
    parts = 4
    share = KC // parts * COMP * BLK
    ccopies = [
        pltpu.make_async_copy(
            cjac.at[pl.ds(p * share, share)], cbuf.at[pl.ds(p * share, share)], csem.at[p]
        )
        for p in range(parts)
    ]
    fcopy = pltpu.make_async_copy(fjac, fbuf, fsem)
    fcopy.start()
    for copy in ccopies:
        copy.start()
    width = COMP * BLK
    rows = jnp.concatenate([cwarm[...], fwarm[...], jnp.zeros((128 - KC - KF, width), f32)], 0)
    rows = jnp.concatenate([rows, jnp.zeros((128, 256 - width), f32)], 1)
    turned = jnp.concatenate([rows[:, :128].T, rows[:, 128:].T], 0)[:width]

    def block(jac, at, k):
        y = jnp.broadcast_to(turned[:, k : k + 1], (width, 128))
        terms_k = jac[at * width : (at + 1) * width, :] * y
        partial[k * 8 : (k + 1) * 8, :] = jnp.sum(terms_k.reshape(width // 8, 8, 128), 0)

    fcopy.wait()
    for m in range(KF):
        block(fbuf, m, KC + m)
    for p, copy in enumerate(ccopies):
        copy.wait()
        for m in range(KC // parts):
            block(cbuf, p * (KC // parts) + m, p * (KC // parts) + m)
    terms[...] = sum(partial[pl.ds(q, KC + KF, stride=8), :] for q in range(8))


def layout_kernel(cjac, fjac, cout, fout, cbuf, fbuf, cturn, fturn, sems, outs):
    copies = [pltpu.make_async_copy(fjac, fbuf, sems.at[0])]
    copies.append(pltpu.make_async_copy(cjac, cbuf, sems.at[1]))
    for copy in copies:
        copy.start()

    def turn(jac, out, parts, depth, first, count):
        k = 128 // parts

        def one(s, _):
            row = s // depth * BLK + s % depth
            rows = [
                jac[pl.ds(row + p * depth, k, stride=COMP * BLK), :] for p in range(parts)
            ]
            out[rows_of(s), :] = jnp.concatenate(rows, 0).T
            return _

        lax.fori_loop(first, first + count, one, 0, unroll=8)

    copies[0].wait()
    turn(fbuf, fturn, GF, IF, 0, SF)
    leaving = [pltpu.make_async_copy(fturn, fout, outs.at[0])]
    leaving[0].start()
    copies[1].wait()
    for part in range(4):
        share = SC // 4
        turn(cbuf, cturn, GC, IC, part * share, share)
        rows = pl.ds(part * share * 128, share * 128)
        copy = pltpu.make_async_copy(cturn.at[rows], cout.at[rows], outs.at[part + 1])
        copy.start()
        leaving.append(copy)
    for copy in leaving:
        copy.wait()


def streamed(jac, buf, sems, slices, work, ahead):
    parts = sems.shape[0]
    share = slices // parts
    copies = []
    for p in range(parts):
        rows = pl.ds(p * share * 128, share * 128)
        copies.append(pltpu.make_async_copy(jac.at[rows], buf.at[rows], sems.at[p]))
    for copy in copies:
        copy.start()
    carry = ahead()
    for p, copy in enumerate(copies):
        copy.wait()
        carry = work(p * share, share, carry)
    return carry


def force_kernel(jac, y, terms, buf, sems):
    total = streamed(
        jac,
        buf,
        sems,
        SC,
        lambda first, count, total: accumulate(buf, y, first, count, total),
        lambda: jnp.zeros((128, 128), f32),
    )
    terms[...] = folded(total, GC)


def scatter_kernel(rows, swap, cterms, fterms, arriving, own, other, total, wide):
    left = left_half(KC)
    near = left_half(KF)
    wide[0:KC, :] = jnp.where(left, cterms[...], 0.0)
    wide[KC : 2 * KC, :] = jnp.where(left, 0.0, cterms[...])
    wide[2 * KC : 2 * KC + KF, :] = jnp.where(near, fterms[...], 0.0)
    wide[2 * KC + KF :, :] = jnp.where(near, 0.0, arriving[...])
    x = wide[...]
    wide[...] = jnp.where(swap[...] > 0, pltpu.roll(x, BLK, 1), x)
    total[...] = jnp.zeros_like(total)
    for m in range(2 * KC + 2 * KF):
        at = pl.ds(rows[m], 1)
        total[at, :] = total[at, :] + wide[m : m + 1, :]
    half = CHIPS * OWN
    own[...] = total[0:half, :].reshape(own.shape)
    other[...] = total[half:, :].reshape(other.shape)


def owner_kernel(with_sums, received, free, mass, last, spread, owned, pieces):
    total = jnp.sum(received[...], 0)
    owned[...] = total
    piece = free[...] + mass[...] * total
    if with_sums:
        change = total - last[...]
        curve = jnp.sum(mass[...] * change * change)
        row = lax.broadcasted_iota(jnp.int32, (8, 128), 0)
        sums = jnp.where(row == 0, jnp.sum(spread[...]), curve)
        piece = jnp.concatenate([piece, sums], 0)
    pieces[...] = jnp.broadcast_to(piece, pieces.shape)


def far_kernel(with_sums, rows, swap, panel, far, *sums):
    base = 2 * KC + KF
    picked = jnp.concatenate([panel[pl.ds(rows[base + m], 1), :] for m in range(KF)], 0)
    far[0:KF, :] = jnp.where(swap[base:, :] > 0, pltpu.roll(picked, BLK, 1), picked)
    if with_sums:
        size = OWN + 8
        total = sum(
            panel[p * size + OWN : (p + 1) * size, :] for p in range(NC * CHIPS)
        )
        sums[0][...] = total
        far[KF:, :] = total


def gradient_kernel(rows, swap, panel, jac, y, live, grad, fown, picked, partial, buf, sems):
    def ahead():
        for m in range(2 * KC + KF):
            picked[m : m + 1, :] = panel[pl.ds(rows[m], 1), :]
        x = picked[...]
        x = jnp.where(swap[0 : 2 * KC + KF, :] > 0, pltpu.roll(x, BLK, 1), x)
        fown[...] = x[2 * KC :]
        joined = jnp.where(left_half(KC), x[0:KC], x[KC : 2 * KC])
        return jnp.concatenate([joined] * GC, 0).T

    def work(first, count, velocity):
        product(buf, velocity, partial, first, count)
        return velocity

    streamed(jac, buf, sems, SC, work, ahead)
    grad[...] = (summed(partial, SC) + regular_weight * y[...]) * live[...]


def cone(pushed, friction):
    normal, first, second = pushed
    tangent = jnp.sqrt(first * first + second * second)
    inside = tangent <= friction * normal
    vanish = friction * tangent <= -normal
    onto = jnp.logical_not(jnp.logical_or(inside, vanish))
    normal_new = (friction * tangent + normal) / (friction * friction + 1.0)
    ratio = jnp.where(onto, friction * normal_new / jnp.where(onto, tangent, 1.0), 1.0)
    keep = jnp.where(inside, 1.0, jnp.where(vanish, 0.0, ratio))
    normal_out = jnp.where(inside, normal, jnp.where(vanish, 0.0, normal_new))
    return jnp.concatenate([normal_out, first * keep, second * keep], 0)


def update_kernel(
    first, beta, last, *refs
):
    (s0, s1, s2, grad, fown, far, jac, cy, fy, cnow, fnow, live, cfric, ffric) = refs[:14]
    (cnew, fnew, cnext, fnext, spread, fterms, partial, buf, sems) = refs[14:]

    def ahead():
        joined = jnp.where(left_half(KF), fown[...], far[0:KF, :])
        return jnp.concatenate([joined] * GF, 0).T

    def work(first_slice, count, velocity):
        product(buf, velocity, partial, first_slice, count)
        return velocity

    streamed(jac, buf, sems, SF, work, ahead)
    fgrad = summed(partial, SF) + regular_weight * fy[...]
    if first:
        step = s0[...]
    else:
        sums = s0[...] + s1[...] + s2[...] + far[KF:, :]
        total = sums[0:1]
        curve = sums[1:2] + regular_weight * total
        step = (total + tiny_sum) / (curve + tiny_sum)

    def project(y, g, friction, depth):
        pushed = y - step * g
        return cone([pushed[c * depth : (c + 1) * depth] for c in range(COMP)], friction)

    cfresh = project(cy[...], grad[...], cfric[...], IC) * live[...]
    ffresh = project(fy[...], fgrad, ffric[...], IF)
    cnew[...] = cfresh
    fnew[...] = ffresh
    if last:
        fnext[...] = ffresh
        cnext[...] = cfresh
        spread[...] = jnp.zeros_like(spread)
    else:
        cafter = cfresh + beta * (cfresh - cnow[...])
        fafter = ffresh + beta * (ffresh - fnow[...])
        cnext[...] = cafter
        fnext[...] = fafter
        cmove, fmove = cafter - cy[...], fafter - fy[...]
        spread[...] = jnp.sum((cmove * cmove).reshape(SC // 8, 8, 128), 0) + jnp.sum(
            (fmove * fmove).reshape(SF // 8, 8, 128), 0
        )
    total = accumulate(buf, fnext, 0, SF, jnp.zeros((128, 128), f32))
    fterms[...] = folded(total, GF)


def exchange(parts):
    groups = [[chip * NC + core for chip in range(CHIPS)] for core in range(NC)]
    return lax.all_to_all(parts, "grp", 0, 0, axis_index_groups=groups, tiled=True)


def all_gather(pieces):
    half = exchange(pieces)
    return jnp.stack([half, other_core(half)]).reshape(-1, 128)


def on_device(
    contact_jac,
    contact_bodies,
    contact_class,
    contact_count,
    face_jac,
    face_own,
    face_far,
    face_class,
    warm_contact,
    warm_face,
    free_velocity,
    inverse_mass,
    friction_table,
    first_step,
):
    free_own = free_velocity.reshape(OWN, 128)
    mass_own = inverse_mass.reshape(OWN, 128)
    slots = jnp.arange(128, dtype=jnp.int32) % KC
    live = (slots < contact_count[0]).astype(f32)[None, :]

    targets = jnp.concatenate(
        [contact_bodies[:, 0], contact_bodies[:, 1], face_own, face_far]
    )
    owner = targets // (2 * OWN)
    slot = (owner - lax.axis_index("grp")) % NC * CHIPS + owner // NC
    row = targets % (2 * OWN) // 2
    sum_rows = slot * OWN + row
    panel_rows = [slot * OWN + row] + [slot * (OWN + 8) + row] * (ITERS - 1)
    order = jnp.arange(targets.shape[0])
    right = ((order >= KC) & (order < 2 * KC)) | (order >= 2 * KC + KF)
    swap = jnp.broadcast_to(
        ((targets % 2 == 1) != right).astype(f32)[:, None], (targets.shape[0], 128)
    )
    cfric = to_lanes(class_lookup(contact_class, friction_table), GC)
    ffric = to_lanes(class_lookup(face_class, friction_table), GF)

    def reduced(cterms, fterms, arriving):
        halves = kernel_call(
            scatter_kernel,
            (shape(CHIPS, OWN, 128), shape(CHIPS, OWN, 128)),
            [smem] + [vmem] * 4,
            [pltpu.VMEM((NC * CHIPS * OWN, 128), f32), pltpu.VMEM((2 * KC + 2 * KF, 128), f32)],
        )(sum_rows, swap, cterms, fterms, arriving)
        return exchange(halves[0] + other_core(halves[1]))

    betas = momentum_weights(ITERS)
    cwarm = warm_contact * live[0, :KC, None]
    crows, frows = contact_jac.reshape(-1, 128), face_jac.reshape(-1, 128)
    cbuf, fbuf = pltpu.VMEM((SC * 128, 128), f32), pltpu.VMEM((SF * 128, 128), f32)
    terms = kernel_call(
        first_force_kernel,
        shape(KC + KF, 128),
        [hbm, hbm, vmem, vmem],
        [
            cbuf,
            fbuf,
            pltpu.VMEM(((KC + KF) * 8, 128), f32),
            pltpu.SemaphoreType.DMA((4,)),
            pltpu.SemaphoreType.DMA,
        ],
        16,
    )(crows, frows, cwarm, warm_face)
    cterms, fterms = terms[:KC], terms[KC:]
    arriving = shifted(fterms, "slab", 1)
    cjac, fjac = kernel_call(
        layout_kernel,
        (shape(SC * 128, 128), shape(SF * 128, 128)),
        [hbm, hbm],
        [cbuf, fbuf, cbuf, fbuf, pltpu.SemaphoreType.DMA((2,)), pltpu.SemaphoreType.DMA((5,))],
        24,
        (hbm, hbm),
    )(crows, frows)
    cnow = to_lanes(cwarm, GC)
    fnow = to_lanes(warm_face, GF)
    cy, fy = cnow, fnow
    spread = jnp.zeros((8, 128), f32)
    owned = free_own
    for turn in range(ITERS):
        received = reduced(cterms, fterms, arriving)
        extra = 8 if turn > 0 else 0
        owned, pieces = kernel_call(
            functools.partial(owner_kernel, turn > 0),
            (shape(OWN, 128), shape(CHIPS, OWN + extra, 128)),
            [vmem] * 5,
        )(received, free_own, mass_own, owned, spread)
        panel = all_gather(pieces)
        picked = kernel_call(
            functools.partial(far_kernel, turn > 0),
            (shape(KF + extra, 128), shape(8, 128))[: 2 if turn > 0 else 1],
            [smem, vmem, vmem],
        )(panel_rows[turn], swap, panel)
        returning = shifted(picked[0], "slab", -1)
        if turn == 0:
            steps = [jnp.broadcast_to(first_step[:, None], (1, 128))] * 3
        else:
            steps = [picked[1]] + [shifted(picked[1], "slab", by) for by in (1, 2)]
        grad, fown = kernel_call(
            gradient_kernel,
            (shape(SC, 128), shape(KF, 128)),
            [smem, vmem, vmem, hbm, vmem, vmem],
            [
                pltpu.VMEM((2 * KC + KF, 128), f32),
                pltpu.VMEM((SC * 8, 128), f32),
                cbuf,
                pltpu.SemaphoreType.DMA((6,)),
            ],
            16,
        )(panel_rows[turn], swap, panel, cjac, cy, live)
        body = functools.partial(update_kernel, turn == 0, betas[turn], turn == ITERS - 1)
        cnow, fnow, cy, fy, spread, fterms = kernel_call(
            body,
            (
                shape(SC, 128),
                shape(SF, 128),
                shape(SC, 128),
                shape(SF, 128),
                shape(8, 128),
                shape(KF, 128),
            ),
            [vmem] * 6 + [hbm] + [vmem] * 7,
            [pltpu.VMEM((SF * 8, 128), f32), fbuf, pltpu.SemaphoreType.DMA((2,))],
        )(*steps, grad, fown, returning, fjac, cy, fy, cnow, fnow, live, cfric, ffric)
        arriving = shifted(fterms, "slab", 1)
        cterms = kernel_call(
            force_kernel,
            shape(KC, 128),
            [hbm, vmem],
            [cbuf, pltpu.SemaphoreType.DMA((6,))],
            16,
        )(cjac, cy)
    received = reduced(cterms, fterms, arriving)
    final = free_own + mass_own * jnp.sum(received, 0)
    return (from_lanes(cnow, GC), from_lanes(fnow, GF), final.reshape(-1))


def solution(mesh):
    return jax.shard_map(
        on_device,
        mesh=mesh,
        in_specs=(
            P(("slab", "grp"), None, None, None),
            P(("slab", "grp"), None),
            P(("slab", "grp"), None),
            P(("slab", "grp")),
            P(("slab", "grp"), None, None, None),
            P(("slab", "grp")),
            P(("slab", "grp")),
            P(("slab", "grp"), None),
            P(("slab", "grp"), None),
            P(("slab", "grp"), None),
            P(("slab", "grp")),
            P(("slab", "grp")),
            P(),
            P(),
        ),
        out_specs=(P(("slab", "grp"), None), P(("slab", "grp"), None), P(("slab", "grp"))),
        check_vma=False,
    )
```

```python
import functools
import math

import jax
import jax.numpy as jnp
from jax import lax
from jax.experimental import pallas as pl
from jax.experimental.pallas import tpu as pltpu
from jax.sharding import PartitionSpec as P

BLK = 64
COMP = 3
ITERS = 3
NY, NZ, NC = 4, 8, 2
CHIPS = NY * NZ
OWN = 16
STRIP = NY * OWN

KC, KF = 64, 16
GC, GF = 128 // KC, 128 // KF
IC, IF = BLK // GC, BLK // GF
SC, SF = COMP * IC, COMP * IF

regular_weight = 0.05
tiny_sum = 1e-06
vmem = pl.BlockSpec(memory_space=pltpu.VMEM)
smem = pl.BlockSpec(memory_space=pltpu.SMEM)
hbm = pl.BlockSpec(memory_space=pltpu.HBM)
f32 = jnp.float32


def shape(*dims):
    return jax.ShapeDtypeStruct(dims, f32)


def kernel_call(body, out, specs, scratch=(), megabytes=4, cost=None):
    return pl.pallas_call(
        body,
        out_shape=out,
        in_specs=specs,
        out_specs=jax.tree.map(lambda _: vmem, out),
        scratch_shapes=list(scratch),
        compiler_params=pltpu.CompilerParams(vmem_limit_bytes=megabytes << 20),
        cost_estimate=cost,
    )


def shifted(x, axis, by):
    devices = lax.axis_size(axis)
    return lax.ppermute(x, axis, [(i, (i + by) % devices) for i in range(devices)])


def other_core(x):
    devices = CHIPS * NC
    return lax.ppermute(x, "grp", [(i, i ^ 1) for i in range(devices)])


def momentum_weights(count):
    theta = 1.0
    weights = []
    for turn in range(count):
        following = (theta * math.sqrt(theta * theta + 4.0) - theta * theta) / 2.0
        weights.append(theta * (1.0 - theta) / (theta * theta + following))
        theta = following
    return weights


def class_lookup(classes, table):
    levels = jnp.arange(table.shape[0], dtype=jnp.int32)
    picked = (classes[:, :, None] == levels).astype(f32)
    return jnp.sum(picked * table, axis=2)


def to_lanes(x, parts):
    k, width = x.shape
    x = x.reshape(k, width // BLK, parts, BLK // parts)
    return x.transpose(1, 3, 2, 0).reshape(width // parts, 128)


def from_lanes(x, parts):
    x = x.reshape(-1, BLK // parts, parts, 128 // parts)
    return x.transpose(3, 0, 2, 1).reshape(128 // parts, -1)


def left_half(rows):
    return lax.broadcasted_iota(jnp.int32, (rows, 128), 1) < BLK


def rows_of(slice_at):
    return pl.ds(pl.multiple_of(slice_at * 128, 128), 128)


def accumulate(jac, y, slices):
    def add(s, total):
        return total + jac[rows_of(s), :] * y[pl.ds(s, 1), :]

    return lax.fori_loop(0, slices, add, jnp.zeros((128, 128), f32), unroll=4)


def folded(total, parts):
    turned = total.T
    k = 128 // parts
    return sum(turned[p * k : (p + 1) * k] for p in range(parts))


def product(jac, velocity, partial, slices):
    def one(s, _):
        terms = jac[rows_of(s), :] * velocity
        partial[pl.ds(pl.multiple_of(s * 8, 8), 8), :] = jnp.sum(
            terms.reshape(16, 8, 128), axis=0
        )
        return _

    lax.fori_loop(0, slices, one, 0, unroll=4)
    return sum(partial[pl.ds(q, slices, stride=8), :] for q in range(8))


def first_force_kernel(cjac, fjac, cwarm, fwarm, terms, cbuf, fbuf, partial, csem, fsem):
    parts = 4
    share = KC // parts * COMP * BLK
    ccopies = [
        pltpu.make_async_copy(
            cjac.at[pl.ds(p * share, share)], cbuf.at[pl.ds(p * share, share)], csem.at[p]
        )
        for p in range(parts)
    ]
    fcopy = pltpu.make_async_copy(fjac, fbuf, fsem)
    fcopy.start()
    for copy in ccopies:
        copy.start()
    width = COMP * BLK
    rows = jnp.concatenate([cwarm[...], fwarm[...], jnp.zeros((128 - KC - KF, width), f32)], 0)
    rows = jnp.concatenate([rows, jnp.zeros((128, 256 - width), f32)], 1)
    turned = jnp.concatenate([rows[:, :128].T, rows[:, 128:].T], 0)[:width]

    def block(jac, at, k):
        y = jnp.broadcast_to(turned[:, k : k + 1], (width, 128))
        terms_k = jac[at * width : (at + 1) * width, :] * y
        partial[k * 8 : (k + 1) * 8, :] = jnp.sum(terms_k.reshape(width // 8, 8, 128), 0)

    fcopy.wait()
    for m in range(KF):
        block(fbuf, m, KC + m)
    for p, copy in enumerate(ccopies):
        copy.wait()
        for m in range(KC // parts):
            block(cbuf, p * (KC // parts) + m, p * (KC // parts) + m)
    terms[...] = sum(partial[pl.ds(q, KC + KF, stride=8), :] for q in range(8))


def layout_kernel(cjac, fjac, after, cout, fout, done, cbuf, fbuf, sems):
    copies = [pltpu.make_async_copy(fjac, fbuf, sems.at[0])]
    copies.append(pltpu.make_async_copy(cjac, cbuf, sems.at[1]))
    for copy in copies:
        copy.start()

    def turn(jac, out, parts, depth, slices):
        k = 128 // parts

        def one(s, _):
            row = s // depth * BLK + s % depth
            rows = [
                jac[pl.ds(row + p * depth, k, stride=COMP * BLK), :] for p in range(parts)
            ]
            out[rows_of(s), :] = jnp.concatenate(rows, 0).T
            return _

        lax.fori_loop(0, slices, one, 0, unroll=8)

    copies[0].wait()
    turn(fbuf, fout, GF, IF, SF)
    copies[1].wait()
    turn(cbuf, cout, GC, IC, SC)
    done[...] = jnp.zeros_like(done)


def force_kernel(jac, y, terms):
    terms[...] = folded(accumulate(jac, y, SC), GC)


def scatter_kernel(rows, swap, cterms, fterms, arriving, own, other, total, wide):
    left = left_half(KC)
    near = left_half(KF)
    wide[0:KC, :] = jnp.where(left, cterms[...], 0.0)
    wide[KC : 2 * KC, :] = jnp.where(left, 0.0, cterms[...])
    wide[2 * KC : 2 * KC + KF, :] = jnp.where(near, fterms[...], 0.0)
    wide[2 * KC + KF :, :] = jnp.where(near, 0.0, arriving[...])
    x = wide[...]
    wide[...] = jnp.where(swap[...] > 0, pltpu.roll(x, BLK, 1), x)
    total[...] = jnp.zeros_like(total)
    for m in range(2 * KC + 2 * KF):
        at = pl.ds(rows[m], 1)
        total[at, :] = total[at, :] + wide[m : m + 1, :]
    half = CHIPS * OWN
    own[...] = total[0:half, :].reshape(own.shape)
    other[...] = total[half:, :].reshape(other.shape)


def strip_kernel(received, spread, after, strip):
    strip[0:STRIP, :] = jnp.sum(received[...], 0)
    strip[STRIP:, :] = jnp.broadcast_to(jnp.sum(spread[...]), (8, 128))


def owner_kernel(with_sums, s0, s1, s2, s3, free, mass, last, total, pieces):
    both = s0[...] + s1[...] + s2[...] + s3[...]
    total[...] = both[0:STRIP]
    piece = free[...] + mass[...] * both[0:STRIP]
    if with_sums:
        change = both[0:STRIP] - last[...]
        curve = jnp.sum(mass[...] * change * change)
        row = lax.broadcasted_iota(jnp.int32, (8, 128), 0)
        piece = jnp.concatenate([piece, jnp.where(row == 0, both[STRIP:], curve)], 0)
    pieces[...] = jnp.broadcast_to(piece, pieces.shape)


def far_kernel(with_sums, rows, swap, panel, far, *sums):
    base = 2 * KC + KF
    picked = jnp.concatenate([panel[pl.ds(rows[base + m], 1), :] for m in range(KF)], 0)
    far[0:KF, :] = jnp.where(swap[base:, :] > 0, pltpu.roll(picked, BLK, 1), picked)
    if with_sums:
        size = STRIP + 8
        total = sum(panel[p * size + STRIP : (p + 1) * size, :] for p in range(NC * NZ))
        sums[0][...] = total
        far[KF:, :] = total


def gradient_kernel(rows, swap, panel, jac, y, live, grad, fown, picked, partial):
    for m in range(2 * KC + KF):
        picked[m : m + 1, :] = panel[pl.ds(rows[m], 1), :]
    x = picked[...]
    x = jnp.where(swap[0 : 2 * KC + KF, :] > 0, pltpu.roll(x, BLK, 1), x)
    fown[...] = x[2 * KC :]
    joined = jnp.where(left_half(KC), x[0:KC], x[KC : 2 * KC])
    velocity = jnp.concatenate([joined] * GC, 0).T
    raw = product(jac, velocity, partial, SC)
    grad[...] = (raw + regular_weight * y[...]) * live[...]


def cone(pushed, friction):
    normal, first, second = pushed
    tangent = jnp.sqrt(first * first + second * second)
    inside = tangent <= friction * normal
    vanish = friction * tangent <= -normal
    onto = jnp.logical_not(jnp.logical_or(inside, vanish))
    normal_new = (friction * tangent + normal) / (friction * friction + 1.0)
    ratio = jnp.where(onto, friction * normal_new / jnp.where(onto, tangent, 1.0), 1.0)
    keep = jnp.where(inside, 1.0, jnp.where(vanish, 0.0, ratio))
    normal_out = jnp.where(inside, normal, jnp.where(vanish, 0.0, normal_new))
    return jnp.concatenate([normal_out, first * keep, second * keep], 0)


def update_kernel(
    first, beta, last, *refs
):
    (s0, s1, s2, grad, fown, far, jac, cy, fy, cnow, fnow, live, cfric, ffric) = refs[:14]
    (cnew, fnew, cnext, fnext, spread, fterms, partial) = refs[14:]
    joined = jnp.where(left_half(KF), fown[...], far[0:KF, :])
    velocity = jnp.concatenate([joined] * GF, 0).T
    fgrad = product(jac, velocity, partial, SF) + regular_weight * fy[...]
    if first:
        step = s0[...]
    else:
        sums = s0[...] + s1[...] + s2[...] + far[KF:, :]
        total = sums[0:1]
        curve = sums[1:2] + regular_weight * total
        step = (total + tiny_sum) / (curve + tiny_sum)

    def project(y, g, friction, depth):
        pushed = y - step * g
        return cone([pushed[c * depth : (c + 1) * depth] for c in range(COMP)], friction)

    cfresh = project(cy[...], grad[...], cfric[...], IC) * live[...]
    ffresh = project(fy[...], fgrad, ffric[...], IF)
    cnew[...] = cfresh
    fnew[...] = ffresh
    if last:
        fnext[...] = ffresh
        cnext[...] = cfresh
        spread[...] = jnp.zeros_like(spread)
    else:
        cafter = cfresh + beta * (cfresh - cnow[...])
        fafter = ffresh + beta * (ffresh - fnow[...])
        cnext[...] = cafter
        fnext[...] = fafter
        cmove, fmove = cafter - cy[...], fafter - fy[...]
        spread[...] = jnp.sum((cmove * cmove).reshape(SC // 8, 8, 128), 0) + jnp.sum(
            (fmove * fmove).reshape(SF // 8, 8, 128), 0
        )
    fterms[...] = folded(accumulate(jac, fnext, SF), GF)


def along_y(x, by):
    line = NZ * NC
    return lax.ppermute(
        x, "grp", [(i, (i + by * line) % (NY * line)) for i in range(NY * line)]
    )


def exchange(parts):
    groups = [
        [(y * NZ + z) * NC + core for z in range(NZ)] for y in range(NY) for core in range(NC)
    ]
    return lax.all_to_all(parts, "grp", 0, 0, axis_index_groups=groups, tiled=True)


def all_gather(pieces):
    half = exchange(pieces)
    return jnp.stack([half, other_core(half)]).reshape(-1, 128)


def on_device(
    contact_jac,
    contact_bodies,
    contact_class,
    contact_count,
    face_jac,
    face_own,
    face_far,
    face_class,
    warm_contact,
    warm_face,
    free_velocity,
    inverse_mass,
    friction_table,
    first_step,
):
    free_own = free_velocity.reshape(OWN, 128)
    mass_own = inverse_mass.reshape(OWN, 128)
    slots = jnp.arange(128, dtype=jnp.int32) % KC
    live = (slots < contact_count[0]).astype(f32)[None, :]

    targets = jnp.concatenate(
        [contact_bodies[:, 0], contact_bodies[:, 1], face_own, face_far]
    )
    owner = targets // (2 * OWN)
    me = lax.axis_index("grp")
    slot = (owner - me) % NC * NZ + owner // NC % NZ
    row = owner // (NC * NZ) * OWN + targets % (2 * OWN) // 2
    sum_rows = slot * STRIP + row
    panel_rows = [slot * STRIP + row] + [slot * (STRIP + 8) + row] * (ITERS - 1)
    my_y = me // (NC * NZ)

    def strip_of(x):
        parts = jnp.stack([x] + [along_y(x, by) for by in range(1, NY)])
        return parts[(my_y - jnp.arange(NY)) % NY].reshape(-1, x.shape[-1])

    constants = strip_of(jnp.concatenate([free_own, mass_own], 1))
    free_strip, mass_strip = constants[:, :128], constants[:, 128:]
    order = jnp.arange(targets.shape[0])
    right = ((order >= KC) & (order < 2 * KC)) | (order >= 2 * KC + KF)
    swap = jnp.broadcast_to(
        ((targets % 2 == 1) != right).astype(f32)[:, None], (targets.shape[0], 128)
    )
    cfric = to_lanes(class_lookup(contact_class, friction_table), GC)
    ffric = to_lanes(class_lookup(face_class, friction_table), GF)

    def core_half(cterms, fterms, arriving):
        halves = kernel_call(
            scatter_kernel,
            (shape(NZ, STRIP, 128), shape(NZ, STRIP, 128)),
            [smem] + [vmem] * 4,
            [pltpu.VMEM((NC * CHIPS * OWN, 128), f32), pltpu.VMEM((2 * KC + 2 * KF, 128), f32)],
        )(sum_rows, swap, cterms, fterms, arriving)
        return halves[0] + other_core(halves[1])

    betas = momentum_weights(ITERS)
    cwarm = warm_contact * live[0, :KC, None]
    crows, frows = contact_jac.reshape(-1, 128), face_jac.reshape(-1, 128)
    cbuf, fbuf = pltpu.VMEM((SC * 128, 128), f32), pltpu.VMEM((SF * 128, 128), f32)
    terms = kernel_call(
        first_force_kernel,
        shape(KC + KF, 128),
        [hbm, hbm, vmem, vmem],
        [
            cbuf,
            fbuf,
            pltpu.VMEM(((KC + KF) * 8, 128), f32),
            pltpu.SemaphoreType.DMA((4,)),
            pltpu.SemaphoreType.DMA,
        ],
        60,
    )(crows, frows, cwarm, warm_face)
    cterms, fterms = terms[:KC], terms[KC:]
    arriving = shifted(fterms, "slab", 1)
    cnow = to_lanes(cwarm, GC)
    fnow = to_lanes(warm_face, GF)
    cy, fy = cnow, fnow
    spread = jnp.zeros((8, 128), f32)
    total = free_strip
    for turn in range(ITERS):
        half = core_half(cterms, fterms, arriving)
        received = exchange(half)
        if turn == 0:
            cjac, fjac, done = kernel_call(
                layout_kernel,
                (shape(SC * 128, 128), shape(SF * 128, 128), shape(8, 128)),
                [hbm, hbm, vmem],
                [cbuf, fbuf, pltpu.SemaphoreType.DMA((2,))],
                20,
                pl.CostEstimate(flops=0, bytes_accessed=40 << 20, transcendentals=0),
            )(crows, frows, half)
        strip = kernel_call(strip_kernel, shape(STRIP + 8, 128), [vmem] * 3)(
            received, spread, done
        )
        strips = [strip] + [along_y(strip, by) for by in range(1, NY)]
        extra = 8 if turn > 0 else 0
        total, pieces = kernel_call(
            functools.partial(owner_kernel, turn > 0),
            (shape(STRIP, 128), shape(NZ, STRIP + extra, 128)),
            [vmem] * 7,
        )(*strips, free_strip, mass_strip, total)
        panel = all_gather(pieces)
        picked = kernel_call(
            functools.partial(far_kernel, turn > 0),
            (shape(KF + extra, 128), shape(8, 128))[: 2 if turn > 0 else 1],
            [smem, vmem, vmem],
        )(panel_rows[turn], swap, panel)
        returning = shifted(picked[0], "slab", -1)
        if turn == 0:
            steps = [jnp.broadcast_to(first_step[:, None], (1, 128))] * 3
        else:
            steps = [picked[1]] + [shifted(picked[1], "slab", by) for by in (1, 2)]
        grad, fown = kernel_call(
            gradient_kernel,
            (shape(SC, 128), shape(KF, 128)),
            [smem] + [vmem] * 5,
            [pltpu.VMEM((2 * KC + KF, 128), f32), pltpu.VMEM((SC * 8, 128), f32)],
        )(panel_rows[turn], swap, panel, cjac, cy, live)
        body = functools.partial(update_kernel, turn == 0, betas[turn], turn == ITERS - 1)
        cnow, fnow, cy, fy, spread, fterms = kernel_call(
            body,
            (
                shape(SC, 128),
                shape(SF, 128),
                shape(SC, 128),
                shape(SF, 128),
                shape(8, 128),
                shape(KF, 128),
            ),
            [vmem] * 14,
            [pltpu.VMEM((SF * 8, 128), f32)],
        )(*steps, grad, fown, returning, fjac, cy, fy, cnow, fnow, live, cfric, ffric)
        arriving = shifted(fterms, "slab", 1)
        cterms = kernel_call(force_kernel, shape(KC, 128), [vmem] * 2)(cjac, cy)
    received = exchange(core_half(cterms, fterms, arriving))
    strip = jnp.sum(received, 0).reshape(NY, OWN, 128)

    def block_at(by):
        return lax.dynamic_index_in_dim(strip, (my_y + by) % NY, 0, keepdims=False)

    owned = block_at(0) + sum(along_y(block_at(by), by) for by in range(1, NY))
    final = free_own + mass_own * owned
    return (from_lanes(cnow, GC), from_lanes(fnow, GF), final.reshape(-1))


def solution(mesh):
    return jax.shard_map(
        on_device,
        mesh=mesh,
        in_specs=(
            P(("slab", "grp"), None, None, None),
            P(("slab", "grp"), None),
            P(("slab", "grp"), None),
            P(("slab", "grp")),
            P(("slab", "grp"), None, None, None),
            P(("slab", "grp")),
            P(("slab", "grp")),
            P(("slab", "grp"), None),
            P(("slab", "grp"), None),
            P(("slab", "grp"), None),
            P(("slab", "grp")),
            P(("slab", "grp")),
            P(),
            P(),
        ),
        out_specs=(P(("slab", "grp"), None), P(("slab", "grp"), None), P(("slab", "grp"))),
        check_vma=False,
    )
```

```python
import functools
import math

import jax
import jax.numpy as jnp
from jax import lax
from jax.experimental import pallas as pl
from jax.experimental.pallas import tpu as pltpu
from jax.sharding import PartitionSpec as P

BLK = 64
COMP = 3
ITERS = 3
NY, NZ, NC = 4, 8, 2
CHIPS = NY * NZ
OWN = 16
HALF = CHIPS * OWN

KC, KF = 64, 16
GC, GF = 128 // KC, 128 // KF
IC, IF = BLK // GC, BLK // GF
SC, SF = COMP * IC, COMP * IF

regular_weight = 0.05
tiny_sum = 1e-06
vmem = pl.BlockSpec(memory_space=pltpu.VMEM)
smem = pl.BlockSpec(memory_space=pltpu.SMEM)
hbm = pl.BlockSpec(memory_space=pltpu.HBM)
f32 = jnp.float32


def shape(*dims):
    return jax.ShapeDtypeStruct(dims, f32)


def kernel_call(
    body, out, specs, scratch=(), megabytes=4, out_specs=None, cost=None, aliases=None
):
    return pl.pallas_call(
        body,
        out_shape=out,
        in_specs=specs,
        out_specs=out_specs or jax.tree.map(lambda _: vmem, out),
        scratch_shapes=list(scratch),
        compiler_params=pltpu.CompilerParams(vmem_limit_bytes=megabytes << 20),
        cost_estimate=cost,
        input_output_aliases=aliases or {},
    )


def shifted(x, axis, by):
    devices = lax.axis_size(axis)
    return lax.ppermute(x, axis, [(i, (i + by) % devices) for i in range(devices)])


def other_core(x):
    devices = CHIPS * NC
    return lax.ppermute(x, "grp", [(i, i ^ 1) for i in range(devices)])


def momentum_weights(count):
    theta = 1.0
    weights = []
    for turn in range(count):
        following = (theta * math.sqrt(theta * theta + 4.0) - theta * theta) / 2.0
        weights.append(theta * (1.0 - theta) / (theta * theta + following))
        theta = following
    return weights


def class_lookup(classes, table):
    levels = jnp.arange(table.shape[0], dtype=jnp.int32)
    picked = (classes[:, :, None] == levels).astype(f32)
    return jnp.sum(picked * table, axis=2)


def to_lanes(x, parts):
    k, width = x.shape
    x = x.reshape(k, width // BLK, parts, BLK // parts)
    return x.transpose(1, 3, 2, 0).reshape(width // parts, 128)


def from_lanes(x, parts):
    x = x.reshape(-1, BLK // parts, parts, 128 // parts)
    return x.transpose(3, 0, 2, 1).reshape(128 // parts, -1)


def left_half(rows):
    return lax.broadcasted_iota(jnp.int32, (rows, 128), 1) < BLK


def rows_of(slice_at):
    return pl.ds(pl.multiple_of(slice_at * 128, 128), 128)


def accumulate(jac, y, slices):
    def add(s, total):
        return total + jac[rows_of(s), :] * y[pl.ds(s, 1), :]

    return lax.fori_loop(0, slices, add, jnp.zeros((128, 128), f32), unroll=4)


def folded(total, parts):
    turned = total.T
    k = 128 // parts
    return sum(turned[p * k : (p + 1) * k] for p in range(parts))


def product(jac, velocity, partial, slices):
    def one(s, _):
        terms = jac[rows_of(s), :] * velocity
        partial[pl.ds(pl.multiple_of(s * 8, 8), 8), :] = jnp.sum(
            terms.reshape(16, 8, 128), axis=0
        )
        return _

    lax.fori_loop(0, slices, one, 0, unroll=4)
    return sum(partial[pl.ds(q, slices, stride=8), :] for q in range(8))


def first_force_kernel(
    cjac, fjac, cwarm, fwarm, cterms, fterms, cbuf, fbuf, partial, csem, fsem
):
    width = COMP * BLK
    parts = ((fjac, fbuf, fsem, KF, KC), (cjac, cbuf, csem, KC, 0))
    copies = []
    for jac, buf, sems, blocks, _ in parts:
        share = blocks // sems.shape[0]
        for p in range(sems.shape[0]):
            rows = pl.ds(p * share * width, share * width)
            copies.append(pltpu.make_async_copy(jac.at[rows], buf.at[rows], sems.at[p]))
    for copy in copies:
        copy.start()
    rows = jnp.concatenate([cwarm[...], fwarm[...], jnp.zeros((128 - KC - KF, width), f32)], 0)
    rows = jnp.concatenate([rows, jnp.zeros((128, 256 - width), f32)], 1)
    turned = jnp.concatenate([rows[:, :128].T, rows[:, 128:].T], 0)[:width]
    for jac, buf, sems, blocks, base in parts:
        share = blocks // sems.shape[0]
        for m in range(blocks):
            if m % share == 0:
                copies.pop(0).wait()
            y = jnp.broadcast_to(turned[:, base + m : base + m + 1], (width, 128))
            products = buf[m * width : (m + 1) * width, :] * y
            partial[(base + m) * 8 : (base + m + 1) * 8, :] = jnp.sum(
                products.reshape(width // 8, 8, 128), 0
            )
    cterms[...] = sum(partial[pl.ds(q, KC, stride=8), :] for q in range(8))
    fterms[...] = sum(partial[pl.ds(KC * 8 + q, KF, stride=8), :] for q in range(8))


def layout_kernel(cjac, fjac, after, cout, fout, done, cbuf, fbuf, cturn, fturn, sems, outs):
    copies = [pltpu.make_async_copy(fjac, fbuf, sems.at[0])]
    for p in range(4):
        rows = pl.ds(p * KC * COMP * BLK // 4, KC * COMP * BLK // 4)
        copies.append(pltpu.make_async_copy(cjac.at[rows], cbuf.at[rows], sems.at[1 + p]))
    for copy in copies:
        copy.start()

    def turn(jac, out, parts, depth, first, count):
        k = 128 // parts

        def one(s, _):
            row = s // depth * BLK + s % depth
            rows = [
                jac[pl.ds(row + p * depth, k, stride=COMP * BLK), :] for p in range(parts)
            ]
            out[rows_of(s), :] = jnp.concatenate(rows, 0).T
            return _

        lax.fori_loop(first, first + count, one, 0, unroll=8)

    copies[0].wait()
    turn(fbuf, fturn, GF, IF, 0, SF)
    leaving = [pltpu.make_async_copy(fturn, fout, outs.at[0])]
    leaving[0].start()
    for copy in copies[1:]:
        copy.wait()
    share = SC // 6
    for part in range(6):
        turn(cbuf, cturn, GC, IC, part * share, share)
        rows = pl.ds(part * share * 128, share * 128)
        leaving.append(pltpu.make_async_copy(cturn.at[rows], cout.at[rows], outs.at[part + 1]))
        leaving[-1].start()
    done[...] = jnp.zeros_like(done)
    for copy in leaving:
        copy.wait()


def force_kernel(jac, y, terms):
    terms[...] = folded(accumulate(jac, y, SC), GC)


def scatter_kernel(rows, swap, cterms, fterms, own, other, total, wide):
    left = left_half(KC)
    count = 2 * KC + KF
    wide[0:KC, :] = jnp.where(left, cterms[...], 0.0)
    wide[KC : 2 * KC, :] = jnp.where(left, 0.0, cterms[...])
    wide[2 * KC :, :] = jnp.where(left_half(KF), fterms[...], 0.0)
    x = wide[...]
    wide[...] = jnp.where(swap[0:count, :] > 0, pltpu.roll(x, BLK, 1), x)
    total[...] = jnp.zeros_like(total)
    for m in range(count):
        at = pl.ds(rows[m], 1)
        total[at, :] = total[at, :] + wide[m : m + 1, :]
    own[...] = total[0:HALF, :]
    other[...] = total[HALF:, :]


def arrive_kernel(rows, swap, arriving, own_in, other_in, own, other, wide):
    base = 2 * KC + KF
    x = jnp.where(left_half(KF), 0.0, arriving[...])
    wide[...] = jnp.where(swap[base:, :] > 0, pltpu.roll(x, BLK, 1), x)
    for m in range(KF):
        row = rows[base + m]
        mine = row < HALF
        value = wide[m : m + 1, :]
        for half, here, at in ((own, mine, row), (other, ~mine, row - HALF)):
            at = pl.ds(jnp.where(here, at, 0), 1)
            half[at, :] = half[at, :] + jnp.where(here, value, 0.0)


def owner_kernel(with_sums, received, free, mass, last, spread, done, owned, pieces):
    total = jnp.sum(received[...], 0)
    owned[...] = total
    piece = free[...] + mass[...] * total
    if with_sums:
        change = total - last[...]
        curve = jnp.sum(mass[...] * change * change)
        row = lax.broadcasted_iota(jnp.int32, (8, 128), 0)
        sums = jnp.where(row == 0, jnp.sum(spread[...]), curve)
        piece = jnp.concatenate([piece, sums], 0)
    pieces[...] = jnp.broadcast_to(piece, pieces.shape)


def far_kernel(with_sums, rows, swap, panel, far, *sums):
    base = 2 * KC + KF
    picked = jnp.concatenate([panel[pl.ds(rows[base + m], 1), :] for m in range(KF)], 0)
    far[0:KF, :] = jnp.where(swap[base:, :] > 0, pltpu.roll(picked, BLK, 1), picked)
    if with_sums:
        size = OWN + 8
        total = sum(panel[p * size + OWN : (p + 1) * size, :] for p in range(NC * CHIPS))
        sums[0][...] = total
        far[KF:, :] = total


def gradient_kernel(rows, swap, panel, jac, y, live, grad, fown, picked, partial):
    for m in range(2 * KC + KF):
        picked[m : m + 1, :] = panel[pl.ds(rows[m], 1), :]
    x = picked[...]
    x = jnp.where(swap[0 : 2 * KC + KF, :] > 0, pltpu.roll(x, BLK, 1), x)
    fown[...] = x[2 * KC :]
    joined = jnp.where(left_half(KC), x[0:KC], x[KC : 2 * KC])
    velocity = jnp.concatenate([joined] * GC, 0).T
    raw = product(jac, velocity, partial, SC)
    grad[...] = (raw + regular_weight * y[...]) * live[...]


def cone(pushed, friction):
    normal, first, second = pushed
    tangent = jnp.sqrt(first * first + second * second)
    inside = tangent <= friction * normal
    vanish = friction * tangent <= -normal
    onto = jnp.logical_not(jnp.logical_or(inside, vanish))
    normal_new = (friction * tangent + normal) / (friction * friction + 1.0)
    ratio = jnp.where(onto, friction * normal_new / jnp.where(onto, tangent, 1.0), 1.0)
    keep = jnp.where(inside, 1.0, jnp.where(vanish, 0.0, ratio))
    normal_out = jnp.where(inside, normal, jnp.where(vanish, 0.0, normal_new))
    return jnp.concatenate([normal_out, first * keep, second * keep], 0)


def update_kernel(
    first, beta, last, *refs
):
    (s0, s1, s2, grad, fown, far, jac, cy, fy, cnow, fnow, live, cfric, ffric) = refs[:14]
    (cnew, fnew, cnext, fnext, spread, fterms, partial) = refs[14:]
    joined = jnp.where(left_half(KF), fown[...], far[0:KF, :])
    velocity = jnp.concatenate([joined] * GF, 0).T
    fgrad = product(jac, velocity, partial, SF) + regular_weight * fy[...]
    if first:
        step = s0[...]
    else:
        sums = s0[...] + s1[...] + s2[...] + far[KF:, :]
        total = sums[0:1]
        curve = sums[1:2] + regular_weight * total
        step = (total + tiny_sum) / (curve + tiny_sum)

    def project(y, g, friction, depth):
        pushed = y - step * g
        return cone([pushed[c * depth : (c + 1) * depth] for c in range(COMP)], friction)

    cfresh = project(cy[...], grad[...], cfric[...], IC) * live[...]
    ffresh = project(fy[...], fgrad, ffric[...], IF)
    cnew[...] = cfresh
    fnew[...] = ffresh
    if last:
        fnext[...] = ffresh
        cnext[...] = cfresh
        spread[...] = jnp.zeros_like(spread)
    else:
        cafter = cfresh + beta * (cfresh - cnow[...])
        fafter = ffresh + beta * (ffresh - fnow[...])
        cnext[...] = cafter
        fnext[...] = fafter
        cmove, fmove = cafter - cy[...], fafter - fy[...]
        spread[...] = jnp.sum((cmove * cmove).reshape(SC // 8, 8, 128), 0) + jnp.sum(
            (fmove * fmove).reshape(SF // 8, 8, 128), 0
        )
    fterms[...] = folded(accumulate(jac, fnext, SF), GF)


def exchange(parts):
    groups = [[chip * NC + core for chip in range(CHIPS)] for core in range(NC)]
    return lax.all_to_all(parts, "grp", 0, 0, axis_index_groups=groups, tiled=True)


def all_gather(pieces):
    half = exchange(pieces)
    return jnp.stack([half, other_core(half)]).reshape(-1, 128)


def on_device(
    contact_jac,
    contact_bodies,
    contact_class,
    contact_count,
    face_jac,
    face_own,
    face_far,
    face_class,
    warm_contact,
    warm_face,
    free_velocity,
    inverse_mass,
    friction_table,
    first_step,
):
    free_own = free_velocity.reshape(OWN, 128)
    mass_own = inverse_mass.reshape(OWN, 128)
    slots = jnp.arange(128, dtype=jnp.int32) % KC
    live = (slots < contact_count[0]).astype(f32)[None, :]

    targets = jnp.concatenate(
        [contact_bodies[:, 0], contact_bodies[:, 1], face_own, face_far]
    )
    owner = targets // (2 * OWN)
    slot = (owner - lax.axis_index("grp")) % NC * CHIPS + owner // NC
    row = targets % (2 * OWN) // 2
    sum_rows = slot * OWN + row
    panel_rows = [slot * OWN + row] + [slot * (OWN + 8) + row] * (ITERS - 1)
    order = jnp.arange(targets.shape[0])
    right = ((order >= KC) & (order < 2 * KC)) | (order >= 2 * KC + KF)
    swap = jnp.broadcast_to(
        ((targets % 2 == 1) != right).astype(f32)[:, None], (targets.shape[0], 128)
    )
    cfric = to_lanes(class_lookup(contact_class, friction_table), GC)
    ffric = to_lanes(class_lookup(face_class, friction_table), GF)

    def core_half(cterms, fterms, arriving):
        own, other = kernel_call(
            scatter_kernel,
            (shape(HALF, 128), shape(HALF, 128)),
            [smem] + [vmem] * 3,
            [pltpu.VMEM((NC * HALF, 128), f32), pltpu.VMEM((2 * KC + KF, 128), f32)],
        )(sum_rows, swap, cterms, fterms)
        own, other = kernel_call(
            arrive_kernel,
            (shape(HALF, 128), shape(HALF, 128)),
            [smem] + [vmem] * 4,
            [pltpu.VMEM((KF, 128), f32)],
            aliases={3: 0, 4: 1},
        )(sum_rows, swap, arriving, own, other)
        return (own + other_core(other)).reshape(CHIPS, OWN, 128)

    betas = momentum_weights(ITERS)
    cwarm = warm_contact * live[0, :KC, None]
    crows, frows = contact_jac.reshape(-1, 128), face_jac.reshape(-1, 128)
    cbuf, fbuf = pltpu.VMEM((SC * 128, 128), f32), pltpu.VMEM((SF * 128, 128), f32)
    cterms, fterms = kernel_call(
        first_force_kernel,
        (shape(KC, 128), shape(KF, 128)),
        [hbm, hbm, vmem, vmem],
        [
            cbuf,
            fbuf,
            pltpu.VMEM(((KC + KF) * 8, 128), f32),
            pltpu.SemaphoreType.DMA((16,)),
            pltpu.SemaphoreType.DMA((4,)),
        ],
        56,
    )(crows, frows, cwarm, warm_face)
    arriving = shifted(fterms, "slab", 1)
    cnow = to_lanes(cwarm, GC)
    fnow = to_lanes(warm_face, GF)
    cy, fy = cnow, fnow
    spread = jnp.zeros((8, 128), f32)
    owned = free_own
    for turn in range(ITERS):
        half = core_half(cterms, fterms, arriving)
        received = exchange(half)
        if turn == 0:
            cjac, fjac, done = kernel_call(
                layout_kernel,
                (shape(SC * 128, 128), shape(SF * 128, 128), shape(8, 128)),
                [hbm, hbm, hbm],
                [
                    cbuf,
                    fbuf,
                    cbuf,
                    fbuf,
                    pltpu.SemaphoreType.DMA((5,)),
                    pltpu.SemaphoreType.DMA((7,)),
                ],
                56,
                (hbm, hbm, vmem),
                pl.CostEstimate(flops=0, bytes_accessed=40 << 20, transcendentals=0),
            )(crows, frows, half[0, 0:8])
        extra = 8 if turn > 0 else 0
        owned, pieces = kernel_call(
            functools.partial(owner_kernel, turn > 0),
            (shape(OWN, 128), shape(CHIPS, OWN + extra, 128)),
            [vmem] * 6,
        )(received, free_own, mass_own, owned, spread, done)
        panel = all_gather(pieces)
        picked = kernel_call(
            functools.partial(far_kernel, turn > 0),
            (shape(KF + extra, 128), shape(8, 128))[: 2 if turn > 0 else 1],
            [smem, vmem, vmem],
        )(panel_rows[turn], swap, panel)
        returning = shifted(picked[0], "slab", -1)
        if turn == 0:
            steps = [jnp.broadcast_to(first_step[:, None], (1, 128))] * 3
        else:
            steps = [picked[1]] + [shifted(picked[1], "slab", by) for by in (1, 2)]
        grad, fown = kernel_call(
            gradient_kernel,
            (shape(SC, 128), shape(KF, 128)),
            [smem] + [vmem] * 5,
            [pltpu.VMEM((2 * KC + KF, 128), f32), pltpu.VMEM((SC * 8, 128), f32)],
        )(panel_rows[turn], swap, panel, cjac, cy, live)
        body = functools.partial(update_kernel, turn == 0, betas[turn], turn == ITERS - 1)
        cnow, fnow, cy, fy, spread, fterms = kernel_call(
            body,
            (
                shape(SC, 128),
                shape(SF, 128),
                shape(SC, 128),
                shape(SF, 128),
                shape(8, 128),
                shape(KF, 128),
            ),
            [vmem] * 14,
            [pltpu.VMEM((SF * 8, 128), f32)],
        )(*steps, grad, fown, returning, fjac, cy, fy, cnow, fnow, live, cfric, ffric)
        arriving = shifted(fterms, "slab", 1)
        cterms = kernel_call(force_kernel, shape(KC, 128), [vmem] * 2)(cjac, cy)
    received = exchange(core_half(cterms, fterms, arriving))
    final = free_own + mass_own * jnp.sum(received, 0)
    return (from_lanes(cnow, GC), from_lanes(fnow, GF), final.reshape(-1))


def solution(mesh):
    return jax.shard_map(
        on_device,
        mesh=mesh,
        in_specs=(
            P(("slab", "grp"), None, None, None),
            P(("slab", "grp"), None),
            P(("slab", "grp"), None),
            P(("slab", "grp")),
            P(("slab", "grp"), None, None, None),
            P(("slab", "grp")),
            P(("slab", "grp")),
            P(("slab", "grp"), None),
            P(("slab", "grp"), None),
            P(("slab", "grp"), None),
            P(("slab", "grp")),
            P(("slab", "grp")),
            P(),
            P(),
        ),
        out_specs=(P(("slab", "grp"), None), P(("slab", "grp"), None), P(("slab", "grp"))),
        check_vma=False,
    )
```

```python
import functools
import math

import jax
import jax.numpy as jnp
from jax import lax
from jax.experimental import pallas as pl
from jax.experimental.pallas import tpu as pltpu
from jax.sharding import PartitionSpec as P

BLK = 64
COMP = 3
ITERS = 3
NY, NZ, NC = 4, 8, 2
CHIPS = NY * NZ
OWN = 16
HALF = CHIPS * OWN

KC, KF = 64, 16
GC, GF = 128 // KC, 128 // KF
IC, IF = BLK // GC, BLK // GF
SC, SF = COMP * IC, COMP * IF

regular_weight = 0.05
tiny_sum = 1e-06
vmem = pl.BlockSpec(memory_space=pltpu.VMEM)
smem = pl.BlockSpec(memory_space=pltpu.SMEM)
hbm = pl.BlockSpec(memory_space=pltpu.HBM)
f32 = jnp.float32


def shape(*dims):
    return jax.ShapeDtypeStruct(dims, f32)


def kernel_call(
    body, out, specs, scratch=(), megabytes=4, out_specs=None, cost=None, aliases=None
):
    return pl.pallas_call(
        body,
        out_shape=out,
        in_specs=specs,
        out_specs=out_specs or jax.tree.map(lambda _: vmem, out),
        scratch_shapes=list(scratch),
        compiler_params=pltpu.CompilerParams(vmem_limit_bytes=megabytes << 20),
        cost_estimate=cost,
        input_output_aliases=aliases or {},
    )


def shifted(x, axis, by):
    devices = lax.axis_size(axis)
    return lax.ppermute(x, axis, [(i, (i + by) % devices) for i in range(devices)])


def other_core(x):
    devices = CHIPS * NC
    return lax.ppermute(x, "grp", [(i, i ^ 1) for i in range(devices)])


def momentum_weights(count):
    theta = 1.0
    weights = []
    for turn in range(count):
        following = (theta * math.sqrt(theta * theta + 4.0) - theta * theta) / 2.0
        weights.append(theta * (1.0 - theta) / (theta * theta + following))
        theta = following
    return weights


def class_lookup(classes, table):
    levels = jnp.arange(table.shape[0], dtype=jnp.int32)
    picked = (classes[:, :, None] == levels).astype(f32)
    return jnp.sum(picked * table, axis=2)


def to_lanes(x, parts):
    k, width = x.shape
    x = x.reshape(k, width // BLK, parts, BLK // parts)
    return x.transpose(1, 3, 2, 0).reshape(width // parts, 128)


def from_lanes(x, parts):
    x = x.reshape(-1, BLK // parts, parts, 128 // parts)
    return x.transpose(3, 0, 2, 1).reshape(128 // parts, -1)


def left_half(rows):
    return lax.broadcasted_iota(jnp.int32, (rows, 128), 1) < BLK


def rows_of(slice_at):
    return pl.ds(pl.multiple_of(slice_at * 128, 128), 128)


def accumulate(jac, y, slices):
    def add(s, total):
        return total + jac[rows_of(s), :] * y[pl.ds(s, 1), :]

    return lax.fori_loop(0, slices, add, jnp.zeros((128, 128), f32), unroll=4)


def folded(total, parts):
    turned = total.T
    k = 128 // parts
    return sum(turned[p * k : (p + 1) * k] for p in range(parts))


def product(jac, velocity, partial, slices):
    def one(s, _):
        terms = jac[rows_of(s), :] * velocity
        partial[pl.ds(pl.multiple_of(s * 8, 8), 8), :] = jnp.sum(
            terms.reshape(16, 8, 128), axis=0
        )
        return _

    lax.fori_loop(0, slices, one, 0, unroll=4)
    return sum(partial[pl.ds(q, slices, stride=8), :] for q in range(8))


def first_force_kernel(cjac, fjac, cwarm, fwarm, cterms, fterms, partial):
    width = COMP * BLK
    rows = jnp.concatenate([cwarm[...], fwarm[...], jnp.zeros((128 - KC - KF, width), f32)], 0)
    rows = jnp.concatenate([rows, jnp.zeros((128, 256 - width), f32)], 1)
    turned = jnp.concatenate([rows[:, :128].T, rows[:, 128:].T], 0)[:width]
    for jac, blocks, base in ((fjac, KF, KC), (cjac, KC, 0)):
        for m in range(blocks):
            y = jnp.broadcast_to(turned[:, base + m : base + m + 1], (width, 128))
            products = jac[m * width : (m + 1) * width, :] * y
            partial[(base + m) * 8 : (base + m + 1) * 8, :] = jnp.sum(
                products.reshape(width // 8, 8, 128), 0
            )
    cterms[...] = sum(partial[pl.ds(q, KC, stride=8), :] for q in range(8))
    fterms[...] = sum(partial[pl.ds(KC * 8 + q, KF, stride=8), :] for q in range(8))


def layout_kernel(cjac, fjac, after, cout, fout, done, cturn, fturn, outs):
    def turn(jac, out, parts, depth, first, count):
        k = 128 // parts

        def one(s, _):
            row = s // depth * BLK + s % depth
            rows = [
                jac[pl.ds(row + p * depth, k, stride=COMP * BLK), :] for p in range(parts)
            ]
            out[rows_of(s), :] = jnp.concatenate(rows, 0).T
            return _

        lax.fori_loop(first, first + count, one, 0, unroll=8)

    turn(fjac, fturn, GF, IF, 0, SF)
    leaving = [pltpu.make_async_copy(fturn, fout, outs.at[0])]
    leaving[0].start()
    share = SC // 6
    for part in range(6):
        turn(cjac, cturn, GC, IC, part * share, share)
        rows = pl.ds(part * share * 128, share * 128)
        leaving.append(pltpu.make_async_copy(cturn.at[rows], cout.at[rows], outs.at[part + 1]))
        leaving[-1].start()
    done[...] = jnp.zeros_like(done)
    for copy in leaving:
        copy.wait()


def force_kernel(jac, y, terms):
    terms[...] = folded(accumulate(jac, y, SC), GC)


def scatter_kernel(rows, swap, cterms, fterms, own, other, total, wide):
    left = left_half(KC)
    count = 2 * KC + KF
    wide[0:KC, :] = jnp.where(left, cterms[...], 0.0)
    wide[KC : 2 * KC, :] = jnp.where(left, 0.0, cterms[...])
    wide[2 * KC :, :] = jnp.where(left_half(KF), fterms[...], 0.0)
    x = wide[...]
    wide[...] = jnp.where(swap[0:count, :] > 0, pltpu.roll(x, BLK, 1), x)
    total[...] = jnp.zeros_like(total)
    for m in range(count):
        at = pl.ds(rows[m], 1)
        total[at, :] = total[at, :] + wide[m : m + 1, :]
    own[...] = total[0:HALF, :]
    other[...] = total[HALF:, :]


def arrive_kernel(rows, swap, arriving, own_in, other_in, own, other, wide):
    base = 2 * KC + KF
    x = jnp.where(left_half(KF), 0.0, arriving[...])
    wide[...] = jnp.where(swap[base:, :] > 0, pltpu.roll(x, BLK, 1), x)
    for m in range(KF):
        row = rows[base + m]
        mine = row < HALF
        value = wide[m : m + 1, :]
        for half, here, at in ((own, mine, row), (other, ~mine, row - HALF)):
            at = pl.ds(jnp.where(here, at, 0), 1)
            half[at, :] = half[at, :] + jnp.where(here, value, 0.0)


def owner_kernel(received, free, mass, last, spread, done, owned, pieces):
    total = jnp.sum(received[...], 0)
    owned[...] = total
    piece = free[...] + mass[...] * total
    change = total - last[...]
    curve = jnp.sum(mass[...] * change * change)
    row = lax.broadcasted_iota(jnp.int32, (2, 128), 0)
    sums = jnp.where(row == 0, jnp.sum(spread[...]), curve)
    pairs = [piece[2 * p : 2 * p + 2] for p in range(OWN // 2)] + [sums]
    pieces[...] = jnp.broadcast_to(jnp.concatenate(pairs, 1)[None], pieces.shape)


def pair_at(panels, slot, pair):
    mine = slot < CHIPS
    chip = jnp.where(mine, slot, slot - CHIPS)
    lanes = pl.ds(pl.multiple_of(pair * 128, 128), 128)
    own, other = (panel[pl.ds(chip, 1), :, lanes] for panel in panels)
    return jnp.where(mine, own, other).reshape(2, 128)


def far_kernel(slots, pairs, odd, swap, own, other, far, sums):
    base = 2 * KC + KF
    picked = [pair_at((own, other), slots[base + m], pairs[base + m]) for m in range(KF)]
    upper = jnp.concatenate([two[0:1] for two in picked], 0)
    lower = jnp.concatenate([two[1:2] for two in picked], 0)
    x = jnp.where(odd[base:, :] > 0, lower, upper)
    far[0:KF, :] = jnp.where(swap[base:, :] > 0, pltpu.roll(x, BLK, 1), x)
    at = OWN // 2 * 128
    total = sum(panel[chip, :, at : at + 128] for panel in (own, other) for chip in range(CHIPS))
    total = jnp.concatenate([total, jnp.zeros((6, 128), f32)], 0)
    sums[...] = total
    far[KF:, :] = total


def gradient_kernel(
    slots, pairs, odd, swap, own, other, jac, y, live, grad, fown, upper, lower, partial
):
    count = 2 * KC + KF
    for m in range(count):
        two = pair_at((own, other), slots[m], pairs[m])
        upper[m : m + 1, :] = two[0:1]
        lower[m : m + 1, :] = two[1:2]
    x = jnp.where(odd[0:count, :] > 0, lower[...], upper[...])
    x = jnp.where(swap[0:count, :] > 0, pltpu.roll(x, BLK, 1), x)
    fown[...] = x[2 * KC :]
    joined = jnp.where(left_half(KC), x[0:KC], x[KC : 2 * KC])
    velocity = jnp.concatenate([joined] * GC, 0).T
    raw = product(jac, velocity, partial, SC)
    grad[...] = (raw + regular_weight * y[...]) * live[...]


def cone(pushed, friction):
    normal, first, second = pushed
    tangent = jnp.sqrt(first * first + second * second)
    inside = tangent <= friction * normal
    vanish = friction * tangent <= -normal
    onto = jnp.logical_not(jnp.logical_or(inside, vanish))
    normal_new = (friction * tangent + normal) / (friction * friction + 1.0)
    ratio = jnp.where(onto, friction * normal_new / jnp.where(onto, tangent, 1.0), 1.0)
    keep = jnp.where(inside, 1.0, jnp.where(vanish, 0.0, ratio))
    normal_out = jnp.where(inside, normal, jnp.where(vanish, 0.0, normal_new))
    return jnp.concatenate([normal_out, first * keep, second * keep], 0)


def update_kernel(
    first, beta, last, *refs
):
    (s0, s1, s2, grad, fown, far, jac, cy, fy, cnow, fnow, live, cfric, ffric) = refs[:14]
    (cnew, fnew, cnext, fnext, spread, fterms, partial) = refs[14:]
    joined = jnp.where(left_half(KF), fown[...], far[0:KF, :])
    velocity = jnp.concatenate([joined] * GF, 0).T
    fgrad = product(jac, velocity, partial, SF) + regular_weight * fy[...]
    if first:
        step = s0[...]
    else:
        sums = s0[...] + s1[...] + s2[...] + far[KF:, :]
        total = sums[0:1]
        curve = sums[1:2] + regular_weight * total
        step = (total + tiny_sum) / (curve + tiny_sum)

    def project(y, g, friction, depth):
        pushed = y - step * g
        return cone([pushed[c * depth : (c + 1) * depth] for c in range(COMP)], friction)

    cfresh = project(cy[...], grad[...], cfric[...], IC) * live[...]
    ffresh = project(fy[...], fgrad, ffric[...], IF)
    cnew[...] = cfresh
    fnew[...] = ffresh
    if last:
        fnext[...] = ffresh
        cnext[...] = cfresh
        spread[...] = jnp.zeros_like(spread)
    else:
        cafter = cfresh + beta * (cfresh - cnow[...])
        fafter = ffresh + beta * (ffresh - fnow[...])
        cnext[...] = cafter
        fnext[...] = fafter
        cmove, fmove = cafter - cy[...], fafter - fy[...]
        spread[...] = jnp.sum((cmove * cmove).reshape(SC // 8, 8, 128), 0) + jnp.sum(
            (fmove * fmove).reshape(SF // 8, 8, 128), 0
        )
    fterms[...] = folded(accumulate(jac, fnext, SF), GF)


def exchange(parts):
    groups = [[chip * NC + core for chip in range(CHIPS)] for core in range(NC)]
    return lax.all_to_all(parts, "grp", 0, 0, axis_index_groups=groups, tiled=True)


def all_gather(pieces):
    half = exchange(pieces)
    return half, other_core(half)


def on_device(
    contact_jac,
    contact_bodies,
    contact_class,
    contact_count,
    face_jac,
    face_own,
    face_far,
    face_class,
    warm_contact,
    warm_face,
    free_velocity,
    inverse_mass,
    friction_table,
    first_step,
):
    free_own = free_velocity.reshape(OWN, 128)
    mass_own = inverse_mass.reshape(OWN, 128)
    slots = jnp.arange(128, dtype=jnp.int32) % KC
    live = (slots < contact_count[0]).astype(f32)[None, :]

    targets = jnp.concatenate(
        [contact_bodies[:, 0], contact_bodies[:, 1], face_own, face_far]
    )
    owner = targets // (2 * OWN)
    slot = (owner - lax.axis_index("grp")) % NC * CHIPS + owner // NC
    row = targets % (2 * OWN) // 2
    sum_rows = slot * OWN + row
    pair = row // 2
    odd = jnp.broadcast_to((row % 2).astype(f32)[:, None], (targets.shape[0], 128))
    order = jnp.arange(targets.shape[0])
    right = ((order >= KC) & (order < 2 * KC)) | (order >= 2 * KC + KF)
    swap = jnp.broadcast_to(
        ((targets % 2 == 1) != right).astype(f32)[:, None], (targets.shape[0], 128)
    )
    cfric = to_lanes(class_lookup(contact_class, friction_table), GC)
    ffric = to_lanes(class_lookup(face_class, friction_table), GF)

    def core_half(cterms, fterms, arriving):
        own, other = kernel_call(
            scatter_kernel,
            (shape(HALF, 128), shape(HALF, 128)),
            [smem] + [vmem] * 3,
            [pltpu.VMEM((NC * HALF, 128), f32), pltpu.VMEM((2 * KC + KF, 128), f32)],
        )(sum_rows, swap, cterms, fterms)
        own, other = kernel_call(
            arrive_kernel,
            (shape(HALF, 128), shape(HALF, 128)),
            [smem] + [vmem] * 4,
            [pltpu.VMEM((KF, 128), f32)],
            aliases={3: 0, 4: 1},
        )(sum_rows, swap, arriving, own, other)
        return (own + other_core(other)).reshape(CHIPS, OWN, 128)

    betas = momentum_weights(ITERS)
    cwarm = warm_contact * live[0, :KC, None]
    crows, frows = contact_jac.reshape(-1, 128), face_jac.reshape(-1, 128)
    cturn, fturn = pltpu.VMEM((SC * 128, 128), f32), pltpu.VMEM((SF * 128, 128), f32)
    cterms, fterms = kernel_call(
        first_force_kernel,
        (shape(KC, 128), shape(KF, 128)),
        [vmem] * 4,
        [pltpu.VMEM(((KC + KF) * 8, 128), f32)],
        10,
    )(crows, frows, cwarm, warm_face)
    arriving = shifted(fterms, "slab", 1)
    cnow = to_lanes(cwarm, GC)
    fnow = to_lanes(warm_face, GF)
    cy, fy = cnow, fnow
    spread = jnp.zeros((8, 128), f32)
    owned = free_own
    for turn in range(ITERS):
        half = core_half(cterms, fterms, arriving)
        received = exchange(half)
        if turn == 0:
            cjac, fjac, done = kernel_call(
                layout_kernel,
                (shape(SC * 128, 128), shape(SF * 128, 128), shape(8, 128)),
                [vmem, vmem, vmem],
                [cturn, fturn, pltpu.SemaphoreType.DMA((7,))],
                52,
                (hbm, hbm, vmem),
                pl.CostEstimate(flops=0, bytes_accessed=40 << 20, transcendentals=0),
            )(crows, frows, half)
        owned, pieces = kernel_call(
            owner_kernel,
            (shape(OWN, 128), shape(CHIPS, 2, (OWN // 2 + 1) * 128)),
            [vmem] * 6,
        )(received, free_own, mass_own, owned, spread, done)
        panels = all_gather(pieces)
        far, slab_sums = kernel_call(
            far_kernel,
            (shape(KF + 8, 128), shape(8, 128)),
            [smem, smem] + [vmem] * 4,
        )(slot, pair, odd, swap, *panels)
        returning = shifted(far, "slab", -1)
        if turn == 0:
            steps = [jnp.broadcast_to(first_step[:, None], (1, 128))] * 3
        else:
            steps = [slab_sums] + [shifted(slab_sums, "slab", by) for by in (1, 2)]
        grad, fown = kernel_call(
            gradient_kernel,
            (shape(SC, 128), shape(KF, 128)),
            [smem, smem] + [vmem] * 7,
            [
                pltpu.VMEM((2 * KC + KF, 128), f32),
                pltpu.VMEM((2 * KC + KF, 128), f32),
                pltpu.VMEM((SC * 8, 128), f32),
            ],
        )(slot, pair, odd, swap, *panels, cjac, cy, live)
        body = functools.partial(update_kernel, turn == 0, betas[turn], turn == ITERS - 1)
        cnow, fnow, cy, fy, spread, fterms = kernel_call(
            body,
            (
                shape(SC, 128),
                shape(SF, 128),
                shape(SC, 128),
                shape(SF, 128),
                shape(8, 128),
                shape(KF, 128),
            ),
            [vmem] * 14,
            [pltpu.VMEM((SF * 8, 128), f32)],
        )(*steps, grad, fown, returning, fjac, cy, fy, cnow, fnow, live, cfric, ffric)
        arriving = shifted(fterms, "slab", 1)
        cterms = kernel_call(force_kernel, shape(KC, 128), [vmem] * 2)(cjac, cy)
    received = exchange(core_half(cterms, fterms, arriving))
    final = free_own + mass_own * jnp.sum(received, 0)
    return (from_lanes(cnow, GC), from_lanes(fnow, GF), final.reshape(-1))


def solution(mesh):
    return jax.shard_map(
        on_device,
        mesh=mesh,
        in_specs=(
            P(("slab", "grp"), None, None, None),
            P(("slab", "grp"), None),
            P(("slab", "grp"), None),
            P(("slab", "grp")),
            P(("slab", "grp"), None, None, None),
            P(("slab", "grp")),
            P(("slab", "grp")),
            P(("slab", "grp"), None),
            P(("slab", "grp"), None),
            P(("slab", "grp"), None),
            P(("slab", "grp")),
            P(("slab", "grp")),
            P(),
            P(),
        ),
        out_specs=(P(("slab", "grp"), None), P(("slab", "grp"), None), P(("slab", "grp"))),
        check_vma=False,
    )
```

```python
import functools
import math

import jax
import jax.numpy as jnp
from jax import lax
from jax.experimental import pallas as pl
from jax.experimental.pallas import tpu as pltpu
from jax.sharding import PartitionSpec as P

BLK = 64
COMP = 3
ITERS = 3
NY, NZ, NC = 4, 8, 2
CHIPS = NY * NZ
OWN = 16
HALF = CHIPS * OWN

KC, KF = 64, 16
GC, GF = 128 // KC, 128 // KF
IC, IF = BLK // GC, BLK // GF
SC, SF = COMP * IC, COMP * IF

regular_weight = 0.05
tiny_sum = 1e-06
vmem = pl.BlockSpec(memory_space=pltpu.VMEM)
smem = pl.BlockSpec(memory_space=pltpu.SMEM)
hbm = pl.BlockSpec(memory_space=pltpu.HBM)
f32 = jnp.float32


def shape(*dims):
    return jax.ShapeDtypeStruct(dims, f32)


def kernel_call(
    body, out, specs, scratch=(), megabytes=4, out_specs=None, cost=None, aliases=None
):
    return pl.pallas_call(
        body,
        out_shape=out,
        in_specs=specs,
        out_specs=out_specs or jax.tree.map(lambda _: vmem, out),
        scratch_shapes=list(scratch),
        compiler_params=pltpu.CompilerParams(vmem_limit_bytes=megabytes << 20),
        cost_estimate=cost,
        input_output_aliases=aliases or {},
    )


def shifted(x, axis, by):
    devices = lax.axis_size(axis)
    return lax.ppermute(x, axis, [(i, (i + by) % devices) for i in range(devices)])


def other_core(x):
    devices = CHIPS * NC
    return lax.ppermute(x, "grp", [(i, i ^ 1) for i in range(devices)])


def momentum_weights(count):
    theta = 1.0
    weights = []
    for turn in range(count):
        following = (theta * math.sqrt(theta * theta + 4.0) - theta * theta) / 2.0
        weights.append(theta * (1.0 - theta) / (theta * theta + following))
        theta = following
    return weights


def class_lookup(classes, table):
    levels = jnp.arange(table.shape[0], dtype=jnp.int32)
    picked = (classes[:, :, None] == levels).astype(f32)
    return jnp.sum(picked * table, axis=2)


def to_lanes(x, parts):
    k, width = x.shape
    x = x.reshape(k, width // BLK, parts, BLK // parts)
    return x.transpose(1, 3, 2, 0).reshape(width // parts, 128)


def from_lanes(x, parts):
    x = x.reshape(-1, BLK // parts, parts, 128 // parts)
    return x.transpose(3, 0, 2, 1).reshape(128 // parts, -1)


def left_half(rows):
    return lax.broadcasted_iota(jnp.int32, (rows, 128), 1) < BLK


def rows_of(slice_at):
    return pl.ds(pl.multiple_of(slice_at * 128, 128), 128)


def accumulate(jac, y, slices):
    def add(s, total):
        return total + jac[rows_of(s), :] * y[pl.ds(s, 1), :]

    return lax.fori_loop(0, slices, add, jnp.zeros((128, 128), f32), unroll=4)


def folded(total, parts):
    turned = total.T
    k = 128 // parts
    return sum(turned[p * k : (p + 1) * k] for p in range(parts))


def product(jac, velocity, partial, slices):
    def one(s, _):
        terms = jac[rows_of(s), :] * velocity
        partial[pl.ds(pl.multiple_of(s * 8, 8), 8), :] = jnp.sum(
            terms.reshape(16, 8, 128), axis=0
        )
        return _

    lax.fori_loop(0, slices, one, 0, unroll=4)
    return sum(partial[pl.ds(q, slices, stride=8), :] for q in range(8))


def first_force_kernel(cjac, fjac, cwarm, fwarm, cterms, fterms, partial):
    width = COMP * BLK
    rows = jnp.concatenate([cwarm[...], fwarm[...], jnp.zeros((128 - KC - KF, width), f32)], 0)
    rows = jnp.concatenate([rows, jnp.zeros((128, 256 - width), f32)], 1)
    turned = jnp.concatenate([rows[:, :128].T, rows[:, 128:].T], 0)[:width]
    for jac, blocks, base in ((fjac, KF, KC), (cjac, KC, 0)):
        for m in range(blocks):
            y = jnp.broadcast_to(turned[:, base + m : base + m + 1], (width, 128))
            products = jac[m * width : (m + 1) * width, :] * y
            partial[(base + m) * 8 : (base + m + 1) * 8, :] = jnp.sum(
                products.reshape(width // 8, 8, 128), 0
            )
    cterms[...] = sum(partial[pl.ds(q, KC, stride=8), :] for q in range(8))
    fterms[...] = sum(partial[pl.ds(KC * 8 + q, KF, stride=8), :] for q in range(8))


def layout_kernel(
    cjac, fjac, after, cout, fout, done, cbuf, fbuf, cturn, fturn, sems, outs
):
    width = COMP * BLK
    copies = [pltpu.make_async_copy(fjac, fbuf, sems.at[COMP])]
    for c in range(COMP):
        rows = pl.ds(c * BLK, BLK)
        copies.append(pltpu.make_async_copy(cjac.at[:, rows], cbuf.at[:, rows], sems.at[c]))
    for copy in copies:
        copy.start()

    def turn(jac, out, parts, depth, first, count):
        k = 128 // parts
        flat = jac.reshape(k * width, 128)

        def one(s, _):
            row = s // depth * BLK + s % depth
            rows = [flat[pl.ds(row + p * depth, k, stride=width), :] for p in range(parts)]
            out[rows_of(s), :] = jnp.concatenate(rows, 0).T
            return _

        lax.fori_loop(first, first + count, one, 0, unroll=8)

    copies[0].wait()
    turn(fbuf, fturn, GF, IF, 0, SF)
    leaving = [pltpu.make_async_copy(fturn, fout, outs.at[COMP])]
    leaving[0].start()
    for c in range(COMP):
        copies[1 + c].wait()
        turn(cbuf, cturn, GC, IC, c * IC, IC)
        rows = pl.ds(c * IC * 128, IC * 128)
        leaving.append(pltpu.make_async_copy(cturn.at[rows], cout.at[rows], outs.at[c]))
        leaving[-1].start()
    done[...] = jnp.zeros_like(done)
    for copy in leaving:
        copy.wait()


def force_kernel(jac, y, terms):
    terms[...] = folded(accumulate(jac, y, SC), GC)


def scatter_kernel(rows, swap, cterms, fterms, own, other, total, wide):
    left = left_half(KC)
    count = 2 * KC + KF
    wide[0:KC, :] = jnp.where(left, cterms[...], 0.0)
    wide[KC : 2 * KC, :] = jnp.where(left, 0.0, cterms[...])
    wide[2 * KC :, :] = jnp.where(left_half(KF), fterms[...], 0.0)
    x = wide[...]
    wide[...] = jnp.where(swap[0:count, :] > 0, pltpu.roll(x, BLK, 1), x)
    total[...] = jnp.zeros_like(total)
    for m in range(count):
        at = pl.ds(rows[m], 1)
        total[at, :] = total[at, :] + wide[m : m + 1, :]
    own[...] = total[0:HALF, :]
    other[...] = total[HALF:, :]


def arrive_kernel(rows, swap, arriving, own_in, other_in, own, other, wide):
    base = 2 * KC + KF
    x = jnp.where(left_half(KF), 0.0, arriving[...])
    wide[...] = jnp.where(swap[base:, :] > 0, pltpu.roll(x, BLK, 1), x)
    for m in range(KF):
        row = rows[base + m]
        mine = row < HALF
        value = wide[m : m + 1, :]
        for half, here, at in ((own, mine, row), (other, ~mine, row - HALF)):
            at = pl.ds(jnp.where(here, at, 0), 1)
            half[at, :] = half[at, :] + jnp.where(here, value, 0.0)


def owner_kernel(received, free, mass, last, spread, done, owned, pieces):
    total = jnp.sum(received[...], 0)
    owned[...] = total
    piece = free[...] + mass[...] * total
    change = total - last[...]
    curve = jnp.sum(mass[...] * change * change)
    row = lax.broadcasted_iota(jnp.int32, (2, 128), 0)
    sums = jnp.where(row == 0, jnp.sum(spread[...]), curve)
    pairs = [piece[2 * p : 2 * p + 2] for p in range(OWN // 2)] + [sums]
    pieces[...] = jnp.broadcast_to(jnp.concatenate(pairs, 1)[None], pieces.shape)


def pick(chips, pairs, odd, afar, panels, scratch, first, count):
    for m in range(count):
        lanes = pl.ds(pl.multiple_of(pairs[first + m] * 128, 128), 128)
        chip = pl.ds(chips[first + m], 1)
        for panel, both in zip(panels, scratch):
            both[2 * m : 2 * m + 2, :] = panel[chip, :, lanes].reshape(2, 128)
    at = pl.ds(first, count)
    lower, other = odd[at, :] > 0, afar[at, :] > 0
    rows = [
        jnp.where(
            lower, both[pl.ds(1, count, stride=2), :], both[pl.ds(0, count, stride=2), :]
        )
        for both in scratch
    ]
    return jnp.where(other, rows[1], rows[0])


def far_kernel(chips, pairs, odd, afar, swap, own, other, far, *scratch):
    base = 2 * KC + KF
    x = pick(chips, pairs, odd, afar, (own, other), scratch, base, KF)
    far[0:KF, :] = jnp.where(swap[base:, :] > 0, pltpu.roll(x, BLK, 1), x)
    at = OWN // 2 * 128
    total = sum(panel[chip, :, at : at + 128] for panel in (own, other) for chip in range(CHIPS))
    far[KF:, :] = jnp.concatenate([total, jnp.zeros((6, 128), f32)], 0)


def gradient_kernel(
    chips, pairs, odd, afar, swap, own, other, sums, jac, y, live, grad, fown, sums_out, *scratch
):
    count = 2 * KC + KF
    x = pick(chips, pairs, odd, afar, (own, other), scratch[:2], 0, count)
    x = jnp.where(swap[0:count, :] > 0, pltpu.roll(x, BLK, 1), x)
    fown[...] = x[2 * KC :]
    joined = jnp.where(left_half(KC), x[0:KC], x[KC : 2 * KC])
    velocity = jnp.concatenate([joined] * GC, 0).T
    raw = product(jac, velocity, scratch[2], SC)
    grad[...] = (raw + regular_weight * y[...]) * live[...]
    sums_out[...] = sums[KF:, :]


def cone(pushed, friction):
    normal, first, second = pushed
    tangent = jnp.sqrt(first * first + second * second)
    inside = tangent <= friction * normal
    vanish = friction * tangent <= -normal
    onto = jnp.logical_not(jnp.logical_or(inside, vanish))
    normal_new = (friction * tangent + normal) / (friction * friction + 1.0)
    ratio = jnp.where(onto, friction * normal_new / jnp.where(onto, tangent, 1.0), 1.0)
    keep = jnp.where(inside, 1.0, jnp.where(vanish, 0.0, ratio))
    normal_out = jnp.where(inside, normal, jnp.where(vanish, 0.0, normal_new))
    return jnp.concatenate([normal_out, first * keep, second * keep], 0)


def update_kernel(
    first, beta, last, *refs
):
    (s0, s1, s2, grad, fown, far, jac, cy, fy, cnow, fnow, live, cfric, ffric) = refs[:14]
    (cnew, fnew, cnext, fnext, spread, fterms, partial) = refs[14:]
    joined = jnp.where(left_half(KF), fown[...], far[0:KF, :])
    velocity = jnp.concatenate([joined] * GF, 0).T
    fgrad = product(jac, velocity, partial, SF) + regular_weight * fy[...]
    if first:
        step = s0[...]
    else:
        sums = s0[...] + s1[...] + s2[...] + far[KF:, :]
        total = sums[0:1]
        curve = sums[1:2] + regular_weight * total
        step = (total + tiny_sum) / (curve + tiny_sum)

    def project(y, g, friction, depth):
        pushed = y - step * g
        return cone([pushed[c * depth : (c + 1) * depth] for c in range(COMP)], friction)

    cfresh = project(cy[...], grad[...], cfric[...], IC) * live[...]
    ffresh = project(fy[...], fgrad, ffric[...], IF)
    cnew[...] = cfresh
    fnew[...] = ffresh
    if last:
        fnext[...] = ffresh
        cnext[...] = cfresh
        spread[...] = jnp.zeros_like(spread)
    else:
        cafter = cfresh + beta * (cfresh - cnow[...])
        fafter = ffresh + beta * (ffresh - fnow[...])
        cnext[...] = cafter
        fnext[...] = fafter
        cmove, fmove = cafter - cy[...], fafter - fy[...]
        spread[...] = jnp.sum((cmove * cmove).reshape(SC // 8, 8, 128), 0) + jnp.sum(
            (fmove * fmove).reshape(SF // 8, 8, 128), 0
        )
    fterms[...] = folded(accumulate(jac, fnext, SF), GF)


def exchange(parts):
    groups = [[chip * NC + core for chip in range(CHIPS)] for core in range(NC)]
    return lax.all_to_all(parts, "grp", 0, 0, axis_index_groups=groups, tiled=True)


def all_gather(pieces):
    half = exchange(pieces)
    return half, other_core(half)


def on_device(
    contact_jac,
    contact_bodies,
    contact_class,
    contact_count,
    face_jac,
    face_own,
    face_far,
    face_class,
    warm_contact,
    warm_face,
    free_velocity,
    inverse_mass,
    friction_table,
    first_step,
):
    free_own = free_velocity.reshape(OWN, 128)
    mass_own = inverse_mass.reshape(OWN, 128)
    slots = jnp.arange(128, dtype=jnp.int32) % KC
    live = (slots < contact_count[0]).astype(f32)[None, :]

    targets = jnp.concatenate(
        [contact_bodies[:, 0], contact_bodies[:, 1], face_own, face_far]
    )
    owner = targets // (2 * OWN)
    slot = (owner - lax.axis_index("grp")) % NC * CHIPS + owner // NC
    row = targets % (2 * OWN) // 2
    sum_rows = slot * OWN + row
    pair = row // 2
    odd = jnp.broadcast_to((row % 2).astype(f32)[:, None], (targets.shape[0], 128))
    afar = jnp.broadcast_to((slot // CHIPS).astype(f32)[:, None], (targets.shape[0], 128))
    chip = slot % CHIPS
    order = jnp.arange(targets.shape[0])
    right = ((order >= KC) & (order < 2 * KC)) | (order >= 2 * KC + KF)
    swap = jnp.broadcast_to(
        ((targets % 2 == 1) != right).astype(f32)[:, None], (targets.shape[0], 128)
    )
    cfric = to_lanes(class_lookup(contact_class, friction_table), GC)
    ffric = to_lanes(class_lookup(face_class, friction_table), GF)

    def core_half(cterms, fterms, arriving):
        own, other = kernel_call(
            scatter_kernel,
            (shape(HALF, 128), shape(HALF, 128)),
            [smem] + [vmem] * 3,
            [pltpu.VMEM((NC * HALF, 128), f32), pltpu.VMEM((2 * KC + KF, 128), f32)],
        )(sum_rows, swap, cterms, fterms)
        own, other = kernel_call(
            arrive_kernel,
            (shape(HALF, 128), shape(HALF, 128)),
            [smem] + [vmem] * 4,
            [pltpu.VMEM((KF, 128), f32)],
            aliases={3: 0, 4: 1},
        )(sum_rows, swap, arriving, own, other)
        return (own + other_core(other)).reshape(CHIPS, OWN, 128)

    betas = momentum_weights(ITERS)
    cwarm = warm_contact * live[0, :KC, None]
    crows, frows = contact_jac.reshape(-1, 128), face_jac.reshape(-1, 128)
    cturn, fturn = pltpu.VMEM((SC * 128, 128), f32), pltpu.VMEM((SF * 128, 128), f32)
    cterms, fterms = kernel_call(
        first_force_kernel,
        (shape(KC, 128), shape(KF, 128)),
        [vmem] * 4,
        [pltpu.VMEM(((KC + KF) * 8, 128), f32)],
        10,
    )(crows, frows, cwarm, warm_face)
    arriving = shifted(fterms, "slab", 1)
    cnow = to_lanes(cwarm, GC)
    fnow = to_lanes(warm_face, GF)
    cy, fy = cnow, fnow
    spread = jnp.zeros((8, 128), f32)
    owned = free_own
    for turn in range(ITERS):
        half = core_half(cterms, fterms, arriving)
        received = exchange(half)
        if turn == 0:
            cjac, fjac, done = kernel_call(
                layout_kernel,
                (shape(SC * 128, 128), shape(SF * 128, 128), shape(8, 128)),
                [hbm, hbm, vmem],
                [
                    pltpu.VMEM((KC, COMP * BLK, 128), f32),
                    pltpu.VMEM((KF, COMP * BLK, 128), f32),
                    cturn,
                    fturn,
                    pltpu.SemaphoreType.DMA((COMP + 1,)),
                    pltpu.SemaphoreType.DMA((COMP + 1,)),
                ],
                54,
                (hbm, hbm, vmem),
                pl.CostEstimate(flops=0, bytes_accessed=40 << 20, transcendentals=0),
            )(
                contact_jac.reshape(KC, COMP * BLK, 128),
                face_jac.reshape(KF, COMP * BLK, 128),
                half,
            )
        owned, pieces = kernel_call(
            owner_kernel,
            (shape(OWN, 128), shape(CHIPS, 2, (OWN // 2 + 1) * 128)),
            [vmem] * 6,
        )(received, free_own, mass_own, owned, spread, done)
        panels = all_gather(pieces)
        far = kernel_call(
            far_kernel,
            shape(KF + 8, 128),
            [smem, smem] + [vmem] * 5,
            [pltpu.VMEM((2 * KF, 128), f32)] * 2,
        )(chip, pair, odd, afar, swap, *panels)
        returning = shifted(far, "slab", -1)
        grad, fown, slab_sums = kernel_call(
            gradient_kernel,
            (shape(SC, 128), shape(KF, 128), shape(8, 128)),
            [smem, smem] + [vmem] * 9,
            [pltpu.VMEM((2 * (2 * KC + KF), 128), f32)] * 2 + [pltpu.VMEM((SC * 8, 128), f32)],
        )(chip, pair, odd, afar, swap, *panels, far, cjac, cy, live)
        if turn == 0:
            steps = [jnp.broadcast_to(first_step[:, None], (1, 128))] * 3
        else:
            steps = [slab_sums] + [shifted(slab_sums, "slab", by) for by in (1, 2)]
        body = functools.partial(update_kernel, turn == 0, betas[turn], turn == ITERS - 1)
        cnow, fnow, cy, fy, spread, fterms = kernel_call(
            body,
            (
                shape(SC, 128),
                shape(SF, 128),
                shape(SC, 128),
                shape(SF, 128),
                shape(8, 128),
                shape(KF, 128),
            ),
            [vmem] * 14,
            [pltpu.VMEM((SF * 8, 128), f32)],
        )(*steps, grad, fown, returning, fjac, cy, fy, cnow, fnow, live, cfric, ffric)
        arriving = shifted(fterms, "slab", 1)
        cterms = kernel_call(force_kernel, shape(KC, 128), [vmem] * 2)(cjac, cy)
    received = exchange(core_half(cterms, fterms, arriving))
    final = free_own + mass_own * jnp.sum(received, 0)
    return (from_lanes(cnow, GC), from_lanes(fnow, GF), final.reshape(-1))


def solution(mesh):
    return jax.shard_map(
        on_device,
        mesh=mesh,
        in_specs=(
            P(("slab", "grp"), None, None, None),
            P(("slab", "grp"), None),
            P(("slab", "grp"), None),
            P(("slab", "grp")),
            P(("slab", "grp"), None, None, None),
            P(("slab", "grp")),
            P(("slab", "grp")),
            P(("slab", "grp"), None),
            P(("slab", "grp"), None),
            P(("slab", "grp"), None),
            P(("slab", "grp")),
            P(("slab", "grp")),
            P(),
            P(),
        ),
        out_specs=(P(("slab", "grp"), None), P(("slab", "grp"), None), P(("slab", "grp"))),
        check_vma=False,
    )
```

```python
import functools
import math

import jax
import jax.numpy as jnp
from jax import lax
from jax.experimental import pallas as pl
from jax.experimental.pallas import tpu as pltpu
from jax.sharding import PartitionSpec as P

BLK = 64
COMP = 3
ITERS = 3
NY, NZ, NC = 4, 8, 2
CHIPS = NY * NZ
OWN = 16
HALF = CHIPS * OWN

KC, KF = 64, 16
GC, GF = 128 // KC, 128 // KF
IC, IF = BLK // GC, BLK // GF
SC, SF = COMP * IC, COMP * IF
PITCH = COMP * BLK + 8

regular_weight = 0.05
tiny_sum = 1e-06
vmem = pl.BlockSpec(memory_space=pltpu.VMEM)
smem = pl.BlockSpec(memory_space=pltpu.SMEM)
hbm = pl.BlockSpec(memory_space=pltpu.HBM)
f32 = jnp.float32


def shape(*dims):
    return jax.ShapeDtypeStruct(dims, f32)


def kernel_call(
    body, out, specs, scratch=(), megabytes=4, out_specs=None, cost=None, aliases=None
):
    return pl.pallas_call(
        body,
        out_shape=out,
        in_specs=specs,
        out_specs=out_specs or jax.tree.map(lambda _: vmem, out),
        scratch_shapes=list(scratch),
        compiler_params=pltpu.CompilerParams(vmem_limit_bytes=megabytes << 20),
        cost_estimate=cost,
        input_output_aliases=aliases or {},
    )


def shifted(x, axis, by):
    devices = lax.axis_size(axis)
    return lax.ppermute(x, axis, [(i, (i + by) % devices) for i in range(devices)])


def other_core(x):
    devices = CHIPS * NC
    return lax.ppermute(x, "grp", [(i, i ^ 1) for i in range(devices)])


def momentum_weights(count):
    theta = 1.0
    weights = []
    for turn in range(count):
        following = (theta * math.sqrt(theta * theta + 4.0) - theta * theta) / 2.0
        weights.append(theta * (1.0 - theta) / (theta * theta + following))
        theta = following
    return weights


def class_lookup(classes, table):
    levels = jnp.arange(table.shape[0], dtype=jnp.int32)
    picked = (classes[:, :, None] == levels).astype(f32)
    return jnp.sum(picked * table, axis=2)


def to_lanes(x, parts):
    k, width = x.shape
    x = x.reshape(k, width // BLK, parts, BLK // parts)
    return x.transpose(1, 3, 2, 0).reshape(width // parts, 128)


def from_lanes(x, parts):
    x = x.reshape(-1, BLK // parts, parts, 128 // parts)
    return x.transpose(3, 0, 2, 1).reshape(128 // parts, -1)


def left_half(rows):
    return lax.broadcasted_iota(jnp.int32, (rows, 128), 1) < BLK


def rows_of(slice_at):
    return pl.ds(pl.multiple_of(slice_at * 128, 128), 128)


def accumulate(jac, y, slices):
    def add(s, total):
        return total + jac[rows_of(s), :] * y[pl.ds(s, 1), :]

    return lax.fori_loop(0, slices, add, jnp.zeros((128, 128), f32), unroll=4)


def folded(total, parts):
    turned = total.T
    k = 128 // parts
    return sum(turned[p * k : (p + 1) * k] for p in range(parts))


def product(jac, velocity, partial, slices):
    def one(s, _):
        terms = jac[rows_of(s), :] * velocity
        partial[pl.ds(pl.multiple_of(s * 8, 8), 8), :] = jnp.sum(
            terms.reshape(16, 8, 128), axis=0
        )
        return _

    lax.fori_loop(0, slices, one, 0, unroll=4)
    return sum(partial[pl.ds(q, slices, stride=8), :] for q in range(8))


def first_force_kernel(cjac, fjac, cwarm, fwarm, cterms, fterms, partial):
    width = COMP * BLK
    rows = jnp.concatenate([cwarm[...], fwarm[...], jnp.zeros((128 - KC - KF, width), f32)], 0)
    rows = jnp.concatenate([rows, jnp.zeros((128, 256 - width), f32)], 1)
    turned = jnp.concatenate([rows[:, :128].T, rows[:, 128:].T], 0)[:width]
    for jac, blocks, base in ((fjac, KF, KC), (cjac, KC, 0)):
        for m in range(blocks):
            y = jnp.broadcast_to(turned[:, base + m : base + m + 1], (width, 128))
            products = jac[m * width : (m + 1) * width, :] * y
            partial[(base + m) * 8 : (base + m + 1) * 8, :] = jnp.sum(
                products.reshape(width // 8, 8, 128), 0
            )
    cterms[...] = sum(partial[pl.ds(q, KC, stride=8), :] for q in range(8))
    fterms[...] = sum(partial[pl.ds(KC * 8 + q, KF, stride=8), :] for q in range(8))


def layout_kernel(
    cjac, fjac, after, cout, fout, done, cbuf, fbuf, cturn, fturn, sems, outs
):
    whole = pl.ds(0, COMP * BLK)
    copies = [pltpu.make_async_copy(fjac, fbuf.at[:, whole], sems.at[COMP])]
    for c in range(COMP):
        rows = pl.ds(c * BLK, BLK)
        copies.append(pltpu.make_async_copy(cjac.at[:, rows], cbuf.at[:, rows], sems.at[c]))
    for copy in copies:
        copy.start()

    def turn(jac, out, parts, depth, first, count):
        k = 128 // parts
        flat = jac.reshape(k * PITCH, 128)

        def one(s, _):
            row = s // depth * BLK + s % depth
            rows = [flat[pl.ds(row + p * depth, k, stride=PITCH), :] for p in range(parts)]
            out[rows_of(s), :] = jnp.concatenate(rows, 0).T
            return _

        lax.fori_loop(first, first + count, one, 0, unroll=8)

    copies[0].wait()
    turn(fbuf, fturn, GF, IF, 0, SF)
    leaving = [pltpu.make_async_copy(fturn, fout, outs.at[COMP])]
    leaving[0].start()
    for c in range(COMP):
        copies[1 + c].wait()
        turn(cbuf, cturn, GC, IC, c * IC, IC)
        rows = pl.ds(c * IC * 128, IC * 128)
        leaving.append(pltpu.make_async_copy(cturn.at[rows], cout.at[rows], outs.at[c]))
        leaving[-1].start()
    done[...] = jnp.zeros_like(done)
    for copy in leaving:
        copy.wait()


def force_kernel(jac, y, terms):
    terms[...] = folded(accumulate(jac, y, SC), GC)


def scatter_kernel(rows, swap, cterms, fterms, own, other, total, wide):
    left = left_half(KC)
    count = 2 * KC + KF
    wide[0:KC, :] = jnp.where(left, cterms[...], 0.0)
    wide[KC : 2 * KC, :] = jnp.where(left, 0.0, cterms[...])
    wide[2 * KC :, :] = jnp.where(left_half(KF), fterms[...], 0.0)
    x = wide[...]
    wide[...] = jnp.where(swap[0:count, :] > 0, pltpu.roll(x, BLK, 1), x)
    total[...] = jnp.zeros_like(total)
    for m in range(count):
        at = pl.ds(rows[m], 1)
        total[at, :] = total[at, :] + wide[m : m + 1, :]
    own[...] = total[0:HALF, :]
    other[...] = total[HALF:, :]


def arrive_kernel(rows, swap, arriving, own_in, other_in, own, other, wide):
    base = 2 * KC + KF
    x = jnp.where(left_half(KF), 0.0, arriving[...])
    wide[...] = jnp.where(swap[base:, :] > 0, pltpu.roll(x, BLK, 1), x)
    for m in range(KF):
        row = rows[base + m]
        mine = row < HALF
        value = wide[m : m + 1, :]
        for half, here, at in ((own, mine, row), (other, ~mine, row - HALF)):
            at = pl.ds(jnp.where(here, at, 0), 1)
            half[at, :] = half[at, :] + jnp.where(here, value, 0.0)


def owner_kernel(received, free, mass, last, spread, done, owned, pieces):
    total = jnp.sum(received[...], 0)
    owned[...] = total
    piece = free[...] + mass[...] * total
    change = total - last[...]
    curve = jnp.sum(mass[...] * change * change)
    row = lax.broadcasted_iota(jnp.int32, (2, 128), 0)
    sums = jnp.where(row == 0, jnp.sum(spread[...]), curve)
    pairs = [piece[2 * p : 2 * p + 2] for p in range(OWN // 2)] + [sums]
    pieces[...] = jnp.broadcast_to(jnp.concatenate(pairs, 1)[None], pieces.shape)


def pick(chips, pairs, odd, afar, panels, scratch, first, count):
    for m in range(count):
        lanes = pl.ds(pl.multiple_of(pairs[first + m] * 128, 128), 128)
        chip = pl.ds(chips[first + m], 1)
        for panel, both in zip(panels, scratch):
            both[2 * m : 2 * m + 2, :] = panel[chip, :, lanes].reshape(2, 128)
    at = pl.ds(first, count)
    lower, other = odd[at, :] > 0, afar[at, :] > 0
    rows = [
        jnp.where(
            lower, both[pl.ds(1, count, stride=2), :], both[pl.ds(0, count, stride=2), :]
        )
        for both in scratch
    ]
    return jnp.where(other, rows[1], rows[0])


def far_kernel(chips, pairs, odd, afar, swap, own, other, far, sums, *scratch):
    base = 2 * KC + KF
    x = pick(chips, pairs, odd, afar, (own, other), scratch, base, KF)
    far[0:KF, :] = jnp.where(swap[base:, :] > 0, pltpu.roll(x, BLK, 1), x)
    at = OWN // 2 * 128
    total = sum(panel[chip, :, at : at + 128] for panel in (own, other) for chip in range(CHIPS))
    total = jnp.concatenate([total, jnp.zeros((6, 128), f32)], 0)
    sums[...] = total
    far[KF:, :] = total


def gradient_kernel(
    chips, pairs, odd, afar, swap, own, other, jac, y, live, grad, fown, *scratch
):
    count = 2 * KC + KF
    x = pick(chips, pairs, odd, afar, (own, other), scratch[:2], 0, count)
    x = jnp.where(swap[0:count, :] > 0, pltpu.roll(x, BLK, 1), x)
    fown[...] = x[2 * KC :]
    joined = jnp.where(left_half(KC), x[0:KC], x[KC : 2 * KC])
    velocity = jnp.concatenate([joined] * GC, 0).T
    raw = product(jac, velocity, scratch[2], SC)
    grad[...] = (raw + regular_weight * y[...]) * live[...]


def cone(pushed, friction):
    normal, first, second = pushed
    tangent = jnp.sqrt(first * first + second * second)
    inside = tangent <= friction * normal
    vanish = friction * tangent <= -normal
    onto = jnp.logical_not(jnp.logical_or(inside, vanish))
    normal_new = (friction * tangent + normal) / (friction * friction + 1.0)
    ratio = jnp.where(onto, friction * normal_new / jnp.where(onto, tangent, 1.0), 1.0)
    keep = jnp.where(inside, 1.0, jnp.where(vanish, 0.0, ratio))
    normal_out = jnp.where(inside, normal, jnp.where(vanish, 0.0, normal_new))
    return jnp.concatenate([normal_out, first * keep, second * keep], 0)


def update_kernel(
    first, beta, last, *refs
):
    (s0, s1, s2, grad, fown, far, jac, cy, fy, cnow, fnow, live, cfric, ffric) = refs[:14]
    (cnew, fnew, cnext, fnext, spread, fterms, partial) = refs[14:]
    joined = jnp.where(left_half(KF), fown[...], far[0:KF, :])
    velocity = jnp.concatenate([joined] * GF, 0).T
    fgrad = product(jac, velocity, partial, SF) + regular_weight * fy[...]
    if first:
        step = s0[...]
    else:
        sums = s0[...] + s1[...] + s2[...] + far[KF:, :]
        total = sums[0:1]
        curve = sums[1:2] + regular_weight * total
        step = (total + tiny_sum) / (curve + tiny_sum)

    def project(y, g, friction, depth):
        pushed = y - step * g
        return cone([pushed[c * depth : (c + 1) * depth] for c in range(COMP)], friction)

    cfresh = project(cy[...], grad[...], cfric[...], IC) * live[...]
    ffresh = project(fy[...], fgrad, ffric[...], IF)
    cnew[...] = cfresh
    fnew[...] = ffresh
    if last:
        fnext[...] = ffresh
        cnext[...] = cfresh
        spread[...] = jnp.zeros_like(spread)
    else:
        cafter = cfresh + beta * (cfresh - cnow[...])
        fafter = ffresh + beta * (ffresh - fnow[...])
        cnext[...] = cafter
        fnext[...] = fafter
        cmove, fmove = cafter - cy[...], fafter - fy[...]
        spread[...] = jnp.sum((cmove * cmove).reshape(SC // 8, 8, 128), 0) + jnp.sum(
            (fmove * fmove).reshape(SF // 8, 8, 128), 0
        )
    fterms[...] = folded(accumulate(jac, fnext, SF), GF)


def exchange(parts):
    groups = [[chip * NC + core for chip in range(CHIPS)] for core in range(NC)]
    return lax.all_to_all(parts, "grp", 0, 0, axis_index_groups=groups, tiled=True)


def all_gather(pieces):
    half = exchange(pieces)
    return half, other_core(half)


def on_device(
    contact_jac,
    contact_bodies,
    contact_class,
    contact_count,
    face_jac,
    face_own,
    face_far,
    face_class,
    warm_contact,
    warm_face,
    free_velocity,
    inverse_mass,
    friction_table,
    first_step,
):
    free_own = free_velocity.reshape(OWN, 128)
    mass_own = inverse_mass.reshape(OWN, 128)
    slots = jnp.arange(128, dtype=jnp.int32) % KC
    live = (slots < contact_count[0]).astype(f32)[None, :]

    targets = jnp.concatenate(
        [contact_bodies[:, 0], contact_bodies[:, 1], face_own, face_far]
    )
    owner = targets // (2 * OWN)
    slot = (owner - lax.axis_index("grp")) % NC * CHIPS + owner // NC
    row = targets % (2 * OWN) // 2
    sum_rows = slot * OWN + row
    pair = row // 2
    odd = jnp.broadcast_to((row % 2).astype(f32)[:, None], (targets.shape[0], 128))
    afar = jnp.broadcast_to((slot // CHIPS).astype(f32)[:, None], (targets.shape[0], 128))
    chip = slot % CHIPS
    order = jnp.arange(targets.shape[0])
    right = ((order >= KC) & (order < 2 * KC)) | (order >= 2 * KC + KF)
    swap = jnp.broadcast_to(
        ((targets % 2 == 1) != right).astype(f32)[:, None], (targets.shape[0], 128)
    )
    cfric = to_lanes(class_lookup(contact_class, friction_table), GC)
    ffric = to_lanes(class_lookup(face_class, friction_table), GF)

    def core_half(cterms, fterms, arriving):
        own, other = kernel_call(
            scatter_kernel,
            (shape(HALF, 128), shape(HALF, 128)),
            [smem] + [vmem] * 3,
            [pltpu.VMEM((NC * HALF, 128), f32), pltpu.VMEM((2 * KC + KF, 128), f32)],
        )(sum_rows, swap, cterms, fterms)
        own, other = kernel_call(
            arrive_kernel,
            (shape(HALF, 128), shape(HALF, 128)),
            [smem] + [vmem] * 4,
            [pltpu.VMEM((KF, 128), f32)],
            aliases={3: 0, 4: 1},
        )(sum_rows, swap, arriving, own, other)
        return (own + other_core(other)).reshape(CHIPS, OWN, 128)

    betas = momentum_weights(ITERS)
    cwarm = warm_contact * live[0, :KC, None]
    crows, frows = contact_jac.reshape(-1, 128), face_jac.reshape(-1, 128)
    cturn, fturn = pltpu.VMEM((SC * 128, 128), f32), pltpu.VMEM((SF * 128, 128), f32)
    cterms, fterms = kernel_call(
        first_force_kernel,
        (shape(KC, 128), shape(KF, 128)),
        [vmem] * 4,
        [pltpu.VMEM(((KC + KF) * 8, 128), f32)],
        10,
    )(crows, frows, cwarm, warm_face)
    arriving = shifted(fterms, "slab", 1)
    cnow = to_lanes(cwarm, GC)
    fnow = to_lanes(warm_face, GF)
    cy, fy = cnow, fnow
    spread = jnp.zeros((8, 128), f32)
    owned = free_own
    for turn in range(ITERS):
        half = core_half(cterms, fterms, arriving)
        received = exchange(half)
        if turn == 0:
            cjac, fjac, done = kernel_call(
                layout_kernel,
                (shape(SC * 128, 128), shape(SF * 128, 128), shape(8, 128)),
                [hbm, hbm, vmem],
                [
                    pltpu.VMEM((KC, PITCH, 128), f32),
                    pltpu.VMEM((KF, PITCH, 128), f32),
                    cturn,
                    fturn,
                    pltpu.SemaphoreType.DMA((COMP + 1,)),
                    pltpu.SemaphoreType.DMA((COMP + 1,)),
                ],
                52,
                (hbm, hbm, vmem),
                pl.CostEstimate(flops=0, bytes_accessed=40 << 20, transcendentals=0),
            )(
                contact_jac.reshape(KC, COMP * BLK, 128),
                face_jac.reshape(KF, COMP * BLK, 128),
                half,
            )
        owned, pieces = kernel_call(
            owner_kernel,
            (shape(OWN, 128), shape(CHIPS, 2, (OWN // 2 + 1) * 128)),
            [vmem] * 5 + [hbm],
        )(received, free_own, mass_own, owned, spread, done)
        panels = all_gather(pieces)
        far, slab_sums = kernel_call(
            far_kernel,
            (shape(KF + 8, 128), shape(8, 128)),
            [smem, smem] + [vmem] * 5,
            [pltpu.VMEM((2 * KF, 128), f32)] * 2,
        )(chip, pair, odd, afar, swap, *panels)
        returning = shifted(far, "slab", -1)
        if turn == 0:
            steps = [jnp.broadcast_to(first_step[:, None], (1, 128))] * 3
        else:
            steps = [slab_sums] + [shifted(slab_sums, "slab", by) for by in (1, 2)]
        grad, fown = kernel_call(
            gradient_kernel,
            (shape(SC, 128), shape(KF, 128)),
            [smem, smem] + [vmem] * 8,
            [pltpu.VMEM((2 * (2 * KC + KF), 128), f32)] * 2 + [pltpu.VMEM((SC * 8, 128), f32)],
        )(chip, pair, odd, afar, swap, *panels, cjac, cy, live)
        body = functools.partial(update_kernel, turn == 0, betas[turn], turn == ITERS - 1)
        cnow, fnow, cy, fy, spread, fterms = kernel_call(
            body,
            (
                shape(SC, 128),
                shape(SF, 128),
                shape(SC, 128),
                shape(SF, 128),
                shape(8, 128),
                shape(KF, 128),
            ),
            [vmem] * 14,
            [pltpu.VMEM((SF * 8, 128), f32)],
        )(*steps, grad, fown, returning, fjac, cy, fy, cnow, fnow, live, cfric, ffric)
        arriving = shifted(fterms, "slab", 1)
        cterms = kernel_call(force_kernel, shape(KC, 128), [vmem] * 2)(cjac, cy)
    received = exchange(core_half(cterms, fterms, arriving))
    final = free_own + mass_own * jnp.sum(received, 0)
    return (from_lanes(cnow, GC), from_lanes(fnow, GF), final.reshape(-1))


def solution(mesh):
    return jax.shard_map(
        on_device,
        mesh=mesh,
        in_specs=(
            P(("slab", "grp"), None, None, None),
            P(("slab", "grp"), None),
            P(("slab", "grp"), None),
            P(("slab", "grp")),
            P(("slab", "grp"), None, None, None),
            P(("slab", "grp")),
            P(("slab", "grp")),
            P(("slab", "grp"), None),
            P(("slab", "grp"), None),
            P(("slab", "grp"), None),
            P(("slab", "grp")),
            P(("slab", "grp")),
            P(),
            P(),
        ),
        out_specs=(P(("slab", "grp"), None), P(("slab", "grp"), None), P(("slab", "grp"))),
        check_vma=False,
    )
```

```python
import functools
import math

import jax
import jax.numpy as jnp
from jax import lax
from jax.experimental import pallas as pl
from jax.experimental.pallas import tpu as pltpu
from jax.sharding import PartitionSpec as P

BLK = 64
COMP = 3
ITERS = 3
NY, NZ, NC = 4, 8, 2
CHIPS = NY * NZ
OWN = 16
HALF = CHIPS * OWN

KC, KF = 64, 16
GC, GF = 128 // KC, 128 // KF
IC, IF = BLK // GC, BLK // GF
SC, SF = COMP * IC, COMP * IF
PITCH = COMP * BLK + 8

regular_weight = 0.05
tiny_sum = 1e-06
vmem = pl.BlockSpec(memory_space=pltpu.VMEM)
smem = pl.BlockSpec(memory_space=pltpu.SMEM)
hbm = pl.BlockSpec(memory_space=pltpu.HBM)
f32 = jnp.float32


def shape(*dims):
    return jax.ShapeDtypeStruct(dims, f32)


def kernel_call(
    body, out, specs, scratch=(), megabytes=4, out_specs=None, cost=None, aliases=None
):
    return pl.pallas_call(
        body,
        out_shape=out,
        in_specs=specs,
        out_specs=out_specs or jax.tree.map(lambda _: vmem, out),
        scratch_shapes=list(scratch),
        compiler_params=pltpu.CompilerParams(vmem_limit_bytes=megabytes << 20),
        cost_estimate=cost,
        input_output_aliases=aliases or {},
    )


def shifted(x, axis, by):
    devices = lax.axis_size(axis)
    return lax.ppermute(x, axis, [(i, (i + by) % devices) for i in range(devices)])


def other_core(x):
    devices = CHIPS * NC
    return lax.ppermute(x, "grp", [(i, i ^ 1) for i in range(devices)])


def momentum_weights(count):
    theta = 1.0
    weights = []
    for turn in range(count):
        following = (theta * math.sqrt(theta * theta + 4.0) - theta * theta) / 2.0
        weights.append(theta * (1.0 - theta) / (theta * theta + following))
        theta = following
    return weights


def class_lookup(classes, table):
    levels = jnp.arange(table.shape[0], dtype=jnp.int32)
    picked = (classes[:, :, None] == levels).astype(f32)
    return jnp.sum(picked * table, axis=2)


def to_lanes(x, parts):
    k, width = x.shape
    x = x.reshape(k, width // BLK, parts, BLK // parts)
    return x.transpose(1, 3, 2, 0).reshape(width // parts, 128)


def from_lanes(x, parts):
    x = x.reshape(-1, BLK // parts, parts, 128 // parts)
    return x.transpose(3, 0, 2, 1).reshape(128 // parts, -1)


def left_half(rows):
    return lax.broadcasted_iota(jnp.int32, (rows, 128), 1) < BLK


def rows_of(slice_at):
    return pl.ds(pl.multiple_of(slice_at * 128, 128), 128)


def accumulate(jac, y, slices):
    def add(s, total):
        return total + jac[rows_of(s), :] * y[pl.ds(s, 1), :]

    return lax.fori_loop(0, slices, add, jnp.zeros((128, 128), f32), unroll=4)


def folded(total, parts):
    turned = total.T
    k = 128 // parts
    return sum(turned[p * k : (p + 1) * k] for p in range(parts))


def product(jac, velocity, partial, slices):
    def one(s, _):
        terms = jac[rows_of(s), :] * velocity
        partial[pl.ds(pl.multiple_of(s * 8, 8), 8), :] = jnp.sum(
            terms.reshape(16, 8, 128), axis=0
        )
        return _

    lax.fori_loop(0, slices, one, 0, unroll=4)
    return sum(partial[pl.ds(q, slices, stride=8), :] for q in range(8))


def first_force_kernel(jac, warm, terms, partial):
    blocks, width = warm.shape
    rows = jnp.concatenate([warm[...], jnp.zeros((128 - blocks, width), f32)], 0)
    rows = jnp.concatenate([rows, jnp.zeros((128, 256 - width), f32)], 1)
    turned = jnp.concatenate([rows[:, :128].T, rows[:, 128:].T], 0)[:width]
    for m in range(blocks):
        y = jnp.broadcast_to(turned[:, m : m + 1], (width, 128))
        products = jac[m * width : (m + 1) * width, :] * y
        partial[m * 8 : (m + 1) * 8, :] = jnp.sum(products.reshape(width // 8, 8, 128), 0)
    terms[...] = sum(partial[pl.ds(q, blocks, stride=8), :] for q in range(8))


def layout_kernel(
    cjac, fjac, after, cout, fout, done, cbuf, fbuf, cturn, fturn, sems, outs
):
    whole = pl.ds(0, COMP * BLK)
    copies = [pltpu.make_async_copy(fjac, fbuf.at[:, whole], sems.at[COMP])]
    for c in range(COMP):
        rows = pl.ds(c * BLK, BLK)
        copies.append(pltpu.make_async_copy(cjac.at[:, rows], cbuf.at[:, rows], sems.at[c]))
    for copy in copies:
        copy.start()

    def turn(jac, out, parts, depth, first, count):
        k = 128 // parts
        flat = jac.reshape(k * PITCH, 128)

        def one(s, _):
            row = s // depth * BLK + s % depth
            rows = [flat[pl.ds(row + p * depth, k, stride=PITCH), :] for p in range(parts)]
            out[rows_of(s), :] = jnp.concatenate(rows, 0).T
            return _

        lax.fori_loop(first, first + count, one, 0, unroll=8)

    copies[0].wait()
    turn(fbuf, fturn, GF, IF, 0, SF)
    leaving = [pltpu.make_async_copy(fturn, fout, outs.at[COMP])]
    leaving[0].start()
    for c in range(COMP):
        copies[1 + c].wait()
        turn(cbuf, cturn, GC, IC, c * IC, IC)
        rows = pl.ds(c * IC * 128, IC * 128)
        leaving.append(pltpu.make_async_copy(cturn.at[rows], cout.at[rows], outs.at[c]))
        leaving[-1].start()
    done[...] = jnp.zeros_like(done)
    for copy in leaving:
        copy.wait()


def force_kernel(jac, y, terms):
    terms[...] = folded(accumulate(jac, y, SC), GC)


def scatter_kernel(rows, swap, cterms, fterms, own, other, total, wide):
    left = left_half(KC)
    count = 2 * KC + KF
    wide[0:KC, :] = jnp.where(left, cterms[...], 0.0)
    wide[KC : 2 * KC, :] = jnp.where(left, 0.0, cterms[...])
    wide[2 * KC :, :] = jnp.where(left_half(KF), fterms[...], 0.0)
    x = wide[...]
    wide[...] = jnp.where(swap[0:count, :] > 0, pltpu.roll(x, BLK, 1), x)
    total[...] = jnp.zeros_like(total)
    for m in range(count):
        at = pl.ds(rows[m], 1)
        total[at, :] = total[at, :] + wide[m : m + 1, :]
    own[...] = total[0:HALF, :]
    other[...] = total[HALF:, :]


def arrive_kernel(rows, swap, arriving, own_in, other_in, own, other, wide):
    base = 2 * KC + KF
    x = jnp.where(left_half(KF), 0.0, arriving[...])
    wide[...] = jnp.where(swap[base:, :] > 0, pltpu.roll(x, BLK, 1), x)
    for m in range(KF):
        row = rows[base + m]
        mine = row < HALF
        value = wide[m : m + 1, :]
        for half, here, at in ((own, mine, row), (other, ~mine, row - HALF)):
            at = pl.ds(jnp.where(here, at, 0), 1)
            half[at, :] = half[at, :] + jnp.where(here, value, 0.0)


def owner_kernel(received, free, mass, last, spread, done, owned, pieces):
    total = jnp.sum(received[...], 0)
    owned[...] = total
    piece = free[...] + mass[...] * total
    change = total - last[...]
    curve = jnp.sum(mass[...] * change * change)
    row = lax.broadcasted_iota(jnp.int32, (2, 128), 0)
    sums = jnp.where(row == 0, jnp.sum(spread[...]), curve)
    pairs = [piece[2 * p : 2 * p + 2] for p in range(OWN // 2)] + [sums]
    pieces[...] = jnp.broadcast_to(jnp.concatenate(pairs, 1)[None], pieces.shape)


def pick(chips, pairs, odd, afar, panels, scratch, first, count):
    for m in range(count):
        lanes = pl.ds(pl.multiple_of(pairs[first + m] * 128, 128), 128)
        chip = pl.ds(chips[first + m], 1)
        for panel, both in zip(panels, scratch):
            both[2 * m : 2 * m + 2, :] = panel[chip, :, lanes].reshape(2, 128)
    at = pl.ds(first, count)
    lower, other = odd[at, :] > 0, afar[at, :] > 0
    rows = [
        jnp.where(
            lower, both[pl.ds(1, count, stride=2), :], both[pl.ds(0, count, stride=2), :]
        )
        for both in scratch
    ]
    return jnp.where(other, rows[1], rows[0])


def far_kernel(chips, pairs, odd, afar, swap, own, other, far, sums, *scratch):
    base = 2 * KC + KF
    x = pick(chips, pairs, odd, afar, (own, other), scratch, base, KF)
    far[0:KF, :] = jnp.where(swap[base:, :] > 0, pltpu.roll(x, BLK, 1), x)
    at = OWN // 2 * 128
    total = sum(panel[chip, :, at : at + 128] for panel in (own, other) for chip in range(CHIPS))
    total = jnp.concatenate([total, jnp.zeros((6, 128), f32)], 0)
    sums[...] = total
    far[KF:, :] = total


def gradient_kernel(
    chips, pairs, odd, afar, swap, own, other, jac, y, live, grad, fown, *scratch
):
    count = 2 * KC + KF
    x = pick(chips, pairs, odd, afar, (own, other), scratch[:2], 0, count)
    x = jnp.where(swap[0:count, :] > 0, pltpu.roll(x, BLK, 1), x)
    fown[...] = x[2 * KC :]
    joined = jnp.where(left_half(KC), x[0:KC], x[KC : 2 * KC])
    velocity = jnp.concatenate([joined] * GC, 0).T
    raw = product(jac, velocity, scratch[2], SC)
    grad[...] = (raw + regular_weight * y[...]) * live[...]


def cone(pushed, friction):
    normal, first, second = pushed
    tangent = jnp.sqrt(first * first + second * second)
    inside = tangent <= friction * normal
    vanish = friction * tangent <= -normal
    onto = jnp.logical_not(jnp.logical_or(inside, vanish))
    normal_new = (friction * tangent + normal) / (friction * friction + 1.0)
    ratio = jnp.where(onto, friction * normal_new / jnp.where(onto, tangent, 1.0), 1.0)
    keep = jnp.where(inside, 1.0, jnp.where(vanish, 0.0, ratio))
    normal_out = jnp.where(inside, normal, jnp.where(vanish, 0.0, normal_new))
    return jnp.concatenate([normal_out, first * keep, second * keep], 0)


def update_kernel(
    first, beta, last, *refs
):
    (s0, s1, s2, grad, fown, far, jac, cy, fy, cnow, fnow, live, cfric, ffric) = refs[:14]
    (cnew, fnew, cnext, fnext, spread, fterms, partial) = refs[14:]
    joined = jnp.where(left_half(KF), fown[...], far[0:KF, :])
    velocity = jnp.concatenate([joined] * GF, 0).T
    fgrad = product(jac, velocity, partial, SF) + regular_weight * fy[...]
    if first:
        step = s0[...]
    else:
        sums = s0[...] + s1[...] + s2[...] + far[KF:, :]
        total = sums[0:1]
        curve = sums[1:2] + regular_weight * total
        step = (total + tiny_sum) / (curve + tiny_sum)

    def project(y, g, friction, depth):
        pushed = y - step * g
        return cone([pushed[c * depth : (c + 1) * depth] for c in range(COMP)], friction)

    cfresh = project(cy[...], grad[...], cfric[...], IC) * live[...]
    ffresh = project(fy[...], fgrad, ffric[...], IF)
    cnew[...] = cfresh
    fnew[...] = ffresh
    if last:
        fnext[...] = ffresh
        cnext[...] = cfresh
        spread[...] = jnp.zeros_like(spread)
    else:
        cafter = cfresh + beta * (cfresh - cnow[...])
        fafter = ffresh + beta * (ffresh - fnow[...])
        cnext[...] = cafter
        fnext[...] = fafter
        cmove, fmove = cafter - cy[...], fafter - fy[...]
        spread[...] = jnp.sum((cmove * cmove).reshape(SC // 8, 8, 128), 0) + jnp.sum(
            (fmove * fmove).reshape(SF // 8, 8, 128), 0
        )
    fterms[...] = folded(accumulate(jac, fnext, SF), GF)


def exchange(parts):
    groups = [[chip * NC + core for chip in range(CHIPS)] for core in range(NC)]
    return lax.all_to_all(parts, "grp", 0, 0, axis_index_groups=groups, tiled=True)


def all_gather(pieces):
    half = exchange(pieces)
    return half, other_core(half)


def on_device(
    contact_jac,
    contact_bodies,
    contact_class,
    contact_count,
    face_jac,
    face_own,
    face_far,
    face_class,
    warm_contact,
    warm_face,
    free_velocity,
    inverse_mass,
    friction_table,
    first_step,
):
    free_own = free_velocity.reshape(OWN, 128)
    mass_own = inverse_mass.reshape(OWN, 128)
    slots = jnp.arange(128, dtype=jnp.int32) % KC
    live = (slots < contact_count[0]).astype(f32)[None, :]

    targets = jnp.concatenate(
        [contact_bodies[:, 0], contact_bodies[:, 1], face_own, face_far]
    )
    owner = targets // (2 * OWN)
    slot = (owner - lax.axis_index("grp")) % NC * CHIPS + owner // NC
    row = targets % (2 * OWN) // 2
    sum_rows = slot * OWN + row
    pair = row // 2
    odd = jnp.broadcast_to((row % 2).astype(f32)[:, None], (targets.shape[0], 128))
    afar = jnp.broadcast_to((slot // CHIPS).astype(f32)[:, None], (targets.shape[0], 128))
    chip = slot % CHIPS
    order = jnp.arange(targets.shape[0])
    right = ((order >= KC) & (order < 2 * KC)) | (order >= 2 * KC + KF)
    swap = jnp.broadcast_to(
        ((targets % 2 == 1) != right).astype(f32)[:, None], (targets.shape[0], 128)
    )
    cfric = to_lanes(class_lookup(contact_class, friction_table), GC)
    ffric = to_lanes(class_lookup(face_class, friction_table), GF)

    def core_half(cterms, fterms, arriving):
        own, other = kernel_call(
            scatter_kernel,
            (shape(HALF, 128), shape(HALF, 128)),
            [smem] + [vmem] * 3,
            [pltpu.VMEM((NC * HALF, 128), f32), pltpu.VMEM((2 * KC + KF, 128), f32)],
        )(sum_rows, swap, cterms, fterms)
        own, other = kernel_call(
            arrive_kernel,
            (shape(HALF, 128), shape(HALF, 128)),
            [smem] + [vmem] * 4,
            [pltpu.VMEM((KF, 128), f32)],
            aliases={3: 0, 4: 1},
        )(sum_rows, swap, arriving, own, other)
        return (own + other_core(other)).reshape(CHIPS, OWN, 128)

    betas = momentum_weights(ITERS)
    cwarm = warm_contact * live[0, :KC, None]
    crows, frows = contact_jac.reshape(-1, 128), face_jac.reshape(-1, 128)
    cturn, fturn = pltpu.VMEM((SC * 128, 128), f32), pltpu.VMEM((SF * 128, 128), f32)
    def first_force(jac, warm):
        blocks = warm.shape[0]
        return kernel_call(
            first_force_kernel,
            shape(blocks, 128),
            [vmem] * 2,
            [pltpu.VMEM((blocks * 8, 128), f32)],
            10,
        )(jac, warm)

    fterms = first_force(frows, warm_face)
    arriving = shifted(fterms, "slab", 1)
    cterms = first_force(crows, cwarm)
    cnow = to_lanes(cwarm, GC)
    fnow = to_lanes(warm_face, GF)
    cy, fy = cnow, fnow
    spread = jnp.zeros((8, 128), f32)
    owned = free_own
    for turn in range(ITERS):
        half = core_half(cterms, fterms, arriving)
        received = exchange(half)
        if turn == 0:
            cjac, fjac, done = kernel_call(
                layout_kernel,
                (shape(SC * 128, 128), shape(SF * 128, 128), shape(8, 128)),
                [hbm, hbm, vmem],
                [
                    pltpu.VMEM((KC, PITCH, 128), f32),
                    pltpu.VMEM((KF, PITCH, 128), f32),
                    cturn,
                    fturn,
                    pltpu.SemaphoreType.DMA((COMP + 1,)),
                    pltpu.SemaphoreType.DMA((COMP + 1,)),
                ],
                52,
                (hbm, hbm, vmem),
                pl.CostEstimate(flops=0, bytes_accessed=40 << 20, transcendentals=0),
            )(
                contact_jac.reshape(KC, COMP * BLK, 128),
                face_jac.reshape(KF, COMP * BLK, 128),
                half,
            )
        owned, pieces = kernel_call(
            owner_kernel,
            (shape(OWN, 128), shape(CHIPS, 2, (OWN // 2 + 1) * 128)),
            [vmem] * 5 + [hbm],
        )(received, free_own, mass_own, owned, spread, done)
        panels = all_gather(pieces)
        far, slab_sums = kernel_call(
            far_kernel,
            (shape(KF + 8, 128), shape(8, 128)),
            [smem, smem] + [vmem] * 5,
            [pltpu.VMEM((2 * KF, 128), f32)] * 2,
        )(chip, pair, odd, afar, swap, *panels)
        returning = shifted(far, "slab", -1)
        if turn == 0:
            steps = [jnp.broadcast_to(first_step[:, None], (1, 128))] * 3
        else:
            steps = [slab_sums] + [shifted(slab_sums, "slab", by) for by in (1, 2)]
        grad, fown = kernel_call(
            gradient_kernel,
            (shape(SC, 128), shape(KF, 128)),
            [smem, smem] + [vmem] * 8,
            [pltpu.VMEM((2 * (2 * KC + KF), 128), f32)] * 2 + [pltpu.VMEM((SC * 8, 128), f32)],
        )(chip, pair, odd, afar, swap, *panels, cjac, cy, live)
        body = functools.partial(update_kernel, turn == 0, betas[turn], turn == ITERS - 1)
        cnow, fnow, cy, fy, spread, fterms = kernel_call(
            body,
            (
                shape(SC, 128),
                shape(SF, 128),
                shape(SC, 128),
                shape(SF, 128),
                shape(8, 128),
                shape(KF, 128),
            ),
            [vmem] * 14,
            [pltpu.VMEM((SF * 8, 128), f32)],
        )(*steps, grad, fown, returning, fjac, cy, fy, cnow, fnow, live, cfric, ffric)
        arriving = shifted(fterms, "slab", 1)
        cterms = kernel_call(force_kernel, shape(KC, 128), [vmem] * 2)(cjac, cy)
    received = exchange(core_half(cterms, fterms, arriving))
    final = free_own + mass_own * jnp.sum(received, 0)
    return (from_lanes(cnow, GC), from_lanes(fnow, GF), final.reshape(-1))


def solution(mesh):
    return jax.shard_map(
        on_device,
        mesh=mesh,
        in_specs=(
            P(("slab", "grp"), None, None, None),
            P(("slab", "grp"), None),
            P(("slab", "grp"), None),
            P(("slab", "grp")),
            P(("slab", "grp"), None, None, None),
            P(("slab", "grp")),
            P(("slab", "grp")),
            P(("slab", "grp"), None),
            P(("slab", "grp"), None),
            P(("slab", "grp"), None),
            P(("slab", "grp")),
            P(("slab", "grp")),
            P(),
            P(),
        ),
        out_specs=(P(("slab", "grp"), None), P(("slab", "grp"), None), P(("slab", "grp"))),
        check_vma=False,
    )
```
